256 devices in a mesh: param: 8 (over y_lo, x), example: 32 (over z, y_hi, core).
Axes of the slice: x: 4, y: 4 (y_hi: 2, y_lo: 2; y = y_hi * 2 + y_lo), z: 8, core: 2. Of those that a mesh axis runs over, the one named last changes fastest.
Arguments:
- acts: bfloat16 [2048, 32, 8192], P('example', None, 'param'), may hold values from -6 to 6
- grads: bfloat16 [2048, 32, 8192], P('example', None, 'param'), may hold values from -6 to 6
- positions: int32 [2048, 24], P('example'), may hold values from 0 to 31, as said below
- proj_in: bfloat16 [8192, 64], P('param'), may hold values from -0.0625 to 0.0625
- proj_out: bfloat16 [8192, 64], P('param'), may hold values from -0.0625 to 0.0625
- window: int32 [32], replicated, may hold values from 0 to 31, each once
Outputs:
- gram: float32 [2048, 2048], P('example', 'param')
The draws below stay inside these ranges and needn't reach their ends.
Inputs may be any that keep to these rules, and one draw needn't show every extreme that they name: The positions of one sequence are distinct.
All inputs are finite; a program needn't handle non-finite values.
Results may differ from the reference program's by a relative error of at most 0.0003.
Values sent between devices are 32-bit elements; how exact they have to be, the bound alone decides.
A program may use at most 64 MiB of HBM per device.

```python
import jax
import jax.numpy as jnp
from jax import lax

D = 8192
K = 64
LEN = 32
LOSS = 24
SEQ_DEV = 64
NBLK = 32
SEQS = 2048


def draw_positions(key, part):
    key = jax.random.fold_in(key, 7)
    keys = jax.random.split(key, SEQS)
    rows = jax.vmap(lambda k: jax.random.permutation(k, LEN)[:LOSS])(keys)
    return rows.astype(jnp.int32)


def block_levels(rng, shape, cuts, low, high):
    loudness = 1.0
    for axis_at, blocks in cuts:
        draws = jax.random.uniform(jax.random.fold_in(jax.random.fold_in(rng, 6), axis_at), (blocks,), jnp.float32, low / len(cuts), high / len(cuts))
        loudness = loudness * jnp.repeat(jnp.exp(draws), shape[axis_at] // blocks).reshape((-1,) + (1,) * (len(shape) - 1 - axis_at))
    return loudness


def gaussian(stream_key, dims, scale, limit, shards=(), kind=jnp.bfloat16):
    level = block_levels(stream_key, dims, shards, -0.22, 0.18) if shards else 1.0
    drawn = jax.random.normal(stream_key, dims, jnp.float32) * scale * level
    return jnp.minimum(jnp.maximum(drawn, -limit), limit).astype(kind)


def setup_inputs(seed: int = 0) -> dict:
    key_of = jax.random.split(jax.random.key(seed), 7)
    acts = gaussian(key_of[0], (SEQS, LEN, D), 1.0, 6.0, ((0, 32), (2, 8)))
    grads = gaussian(key_of[1], (SEQS, LEN, D), 1.0, 6.0, ((0, 32), (2, 8)))
    positions = draw_positions(jax.random.fold_in(key_of[6], 71), 0)
    proj_in = gaussian(key_of[3], (D, K), D ** -0.5, 0.0625, ((0, 8),))
    proj_out = gaussian(key_of[4], (D, K), D ** -0.5, 0.0625, ((0, 8),))
    window = jax.random.permutation(key_of[5], NBLK).astype(jnp.int32)
    return {"acts": acts, "grads": grads, "positions": positions, "proj_in": proj_in, "proj_out": proj_out, "window": window}


def reference(acts, grads, positions, proj_in, proj_out, window):
    picked = positions[:, :, None]
    xs = jnp.take_along_axis(acts, picked, axis=1).reshape(-1, D)
    gs = jnp.take_along_axis(grads, picked, axis=1).reshape(-1, D)
    left = jnp.dot(xs, proj_in, preferred_element_type=jnp.float32).reshape(SEQS, LOSS, K)
    right = jnp.dot(gs, proj_out, preferred_element_type=jnp.float32).reshape(SEQS, LOSS, K)
    feats = jnp.einsum("sti,stj->sij", right, left, precision=lax.Precision.HIGHEST).reshape(SEQS, K * K)
    ordered = jnp.take(feats.reshape(NBLK, SEQ_DEV, K * K), window, axis=0).reshape(SEQS, K * K)
    return jnp.dot(feats, ordered.T, precision=lax.Precision.HIGHEST, preferred_element_type=jnp.float32)
```

```python
import jax
import jax.numpy as jnp
from jax import lax
from jax.experimental import pallas as pl
from jax.experimental.pallas import tpu as pltpu
from jax.sharding import PartitionSpec as P

F32, BF16 = jnp.float32, jnp.bfloat16
MESH = pl.DeviceIdType.MESH

NP, NX, NY, NZ, NC = 8, 4, 4, 8, 2
SEQ, LEN, LOSS, RANK = 64, 32, 24, 64
OWN = SEQ // NP
WIN = NZ * NY // 2 * NC
TOK = OWN * LEN
PICK = OWN * LOSS
HALF = RANK // 2
FPZ = HALF // NZ
ROWS = NX * OWN
COLS = WIN * 2 * OWN


def iota(shape, dim):
    return lax.broadcasted_iota(jnp.int32, shape, dim)


def split(v):
    hi = v.astype(BF16)
    return hi, (v - hi.astype(F32)).astype(BF16)


def mm(a, b, dims=((1,), (0,))):
    return lax.dot_general(a, b, (dims, ((), ())), preferred_element_type=F32)


NT = ((1,), (1,))


def kernel(
    acts, grads, pos, w_in, w_out, window, out,
    xbuf, gbuf, wbuf, sbuf, rbuf, fbuf, rowbuf, colbuf,
    lhs_hi, lhs_lo, rhs_hi, rhs_lo, pbuf, prec, qsend, qrecv,
    in_sem, loc_sem, a_s, a_r, z_s, z_r, x_s, x_r, y_s, y_r, c_s, c_r, g_s, g_r, f_s, f_r,
):
    p, e = lax.axis_index("param"), lax.axis_index("example")
    yl, x = p // NX, p % NX
    z, yh, c = e // 4, (e // 2) % 2, e % 2
    y = yh * 2 + yl

    def dev(p_=None, e_=None):
        return {"param": p if p_ is None else p_, "example": e if e_ is None else e_}

    def at_p(k):
        return dev(p_=(p + k) % NP)

    def at_z(k):
        return dev(e_=((z + k) % NZ) * 4 + yh * 2 + c)

    def at_x(k):
        return dev(p_=yl * NX + (x + k) % NX)

    def at_y(k):
        y_ = (y + k) % NY
        return dev(p_=(y_ % 2) * NX + x, e_=z * 4 + (y_ // 2) * 2 + c)

    partner = dev(e_=z * 4 + yh * 2 + (1 - c))

    def fetch(q, i):
        src, dst = (acts, xbuf) if i == 0 else (grads, gbuf)
        return pltpu.make_async_copy(
            src.at[pl.ds(pl.multiple_of(q * OWN, OWN), OWN)], dst.at[q], in_sem.at[i, q]
        )

    for k in range(1, NP + 1):
        q = (p + k) % NP
        fetch(q, 0).start()
        fetch(q, 1).start()

    barrier = pltpu.get_barrier_semaphore()
    others = [at_p(k) for k in range(1, NP)] + [at_z(k) for k in range(1, NZ)]
    others += [at_y(1), at_y(2), at_y(3), partner]
    for d in others:
        pl.semaphore_signal(barrier, inc=1, device_id=d, device_id_type=MESH)

    zero = jnp.zeros((w_in.shape[0], RANK), BF16)
    wbuf[0] = jnp.concatenate([w_in[...], zero], axis=1)
    wbuf[1] = jnp.concatenate([zero, w_out[...]], axis=1)
    pick_t = (iota((PICK, LOSS), 0) % LOSS == iota((PICK, LOSS), 1)).astype(BF16)
    pos_t = mm(pick_t, pos[...].astype(F32).astype(BF16), NT).astype(BF16)
    lane = iota((PICK, TOK), 1)
    own_seq = iota((PICK, TOK), 0) // LOSS == lane // LEN
    token = jnp.where(own_seq, lane % LEN, -1).astype(F32)
    spread_at = iota((SEQ, TOK), 0) - iota((SEQ, TOK), 1) // LEN

    def project(q):
        fetch(q, 0).wait()
        fetch(q, 1).wait()
        ab = mm(xbuf[q].reshape(TOK, -1), wbuf[0]) + mm(gbuf[q].reshape(TOK, -1), wbuf[1])
        spread = (spread_at == q * OWN).astype(F32).astype(BF16)
        one_hot = (mm(pos_t, spread) == token).astype(F32).astype(BF16)
        hi, lo = split(ab)
        return mm(one_hot, hi) + mm(one_hot, lo)

    def send_part(k):
        q = (p + k) % NP
        return pltpu.make_async_remote_copy(
            sbuf.at[q], rbuf.at[p], a_s.at[q], a_r.at[p], device_id=dev(p_=q), device_id_type=MESH
        )

    sbuf[(p + 1) % NP] = project((p + 1) % NP)
    pl.semaphore_wait(barrier, len(others))
    send_part(1).start()

    def step(k, _):
        q = (p + k) % NP
        sbuf[q] = project(q)
        send_part(k).start()
        return 0

    lax.fori_loop(2, NP, step, 0)
    rbuf[p] = project(p)

    def recv_part(q):
        return pltpu.make_async_remote_copy(
            sbuf.at[q], rbuf.at[q], a_s.at[q], a_r.at[q], device_id=dev(p_=q), device_id_type=MESH
        )

    for k in range(1, NP):
        recv_part((p + k) % NP).wait_recv()
    total = rbuf[0]
    for q in range(1, NP):
        total = total + rbuf[q]

    b_t = total.T[RANK:]
    in_seq = iota((OWN, PICK), 1) // LOSS == iota((OWN, PICK), 0)
    a_low = jnp.where(iota((PICK, 2 * RANK), 1) < RANK, total, 0.0)
    feats = jnp.zeros((HALF * OWN, 2 * RANK), F32)
    for h in range(2):
        b_h = b_t[h * HALF : (h + 1) * HALF]
        b_hi, b_lo = split(jnp.where(in_seq[None], b_h[:, None, :], 0.0).reshape(HALF * OWN, PICK))
        a_hi, a_lo = split(a_low if h == 0 else pltpu.roll(a_low, RANK, 1))
        feats = feats + (mm(b_hi, a_hi) + (mm(b_hi, a_lo) + mm(b_lo, a_hi)))
    fbuf[...] = feats.reshape(HALF, OWN, 2 * RANK)

    def tiles(k):
        z_ = (z + k) % NZ
        return pltpu.make_async_remote_copy(
            fbuf.at[pl.ds(z_ * FPZ, FPZ)], rowbuf.at[x, :, z], z_s.at[k], z_r.at[k],
            device_id=at_z(k), device_id_type=MESH,
        )

    for k in (4, 3, 5, 2, 6, 1, 7):
        tiles(k).start()
    rowbuf[x, :, z] = fbuf[pl.ds(z * FPZ, FPZ)]
    for k in range(1, NZ):
        tiles(k).wait_recv()

    def to_x(k):
        return pltpu.make_async_remote_copy(
            rowbuf.at[x], rowbuf.at[x], x_s.at[k], x_r.at[k], device_id=at_x(k), device_id_type=MESH
        )

    def from_x(k):
        x_ = (x + NX - k) % NX
        return pltpu.make_async_remote_copy(
            rowbuf.at[x_], rowbuf.at[x_], x_s.at[k], x_r.at[k], device_id=at_x(k), device_id_type=MESH
        )

    def to_y(k):
        return pltpu.make_async_remote_copy(
            rowbuf.at[x], colbuf.at[y, c], y_s.at[k], y_r.at[k], device_id=at_y(k), device_id_type=MESH
        )

    def from_y(k):
        y_ = (y + NY - k) % NY
        return pltpu.make_async_remote_copy(
            rowbuf.at[x], colbuf.at[y_, c], y_s.at[k], y_r.at[k], device_id=at_y(k), device_id_type=MESH
        )

    def to_core(k):
        y_ = (y + NY - k) % NY
        src = rowbuf.at[x] if k == 0 else colbuf.at[y_, c]
        return pltpu.make_async_remote_copy(
            src, colbuf.at[y_, c], c_s.at[k], c_r.at[k], device_id=partner, device_id_type=MESH
        )

    def from_core(k):
        y_ = (y + NY - k) % NY
        return pltpu.make_async_remote_copy(
            rowbuf.at[x], colbuf.at[y_, 1 - c], c_s.at[k], c_r.at[k], device_id=partner, device_id_type=MESH
        )

    own_cols = pltpu.make_async_copy(rowbuf.at[x], colbuf.at[y, c], loc_sem.at[0])
    for k in (2, 1, 3):
        to_y(k).start()
        to_x(k).start()
    to_core(0).start()
    own_cols.start()
    for k in (1, 3, 2):
        from_y(k).wait_recv()
        to_core(k).start()
    for k in (1, 3, 2):
        from_x(k).wait_recv()
    for i in range(FPZ):
        for z_ in range(NZ):
            hi, lo = split(rowbuf[:, i, z_].reshape(ROWS, 2 * RANK))
            at = (pl.ds(z_ * ROWS, ROWS), pl.ds(i * 2 * RANK, 2 * RANK))
            lhs_hi[at] = hi
            lhs_lo[at] = lo
    own_cols.wait()
    for k in range(NY):
        from_core(k).wait_recv()

    def column_block(w, _):
        e_ = window[w]
        z_, yh_, c_ = e_ // 4, (e_ // 2) % 2, e_ % 2
        for i in range(FPZ):
            v = jnp.concatenate(
                [colbuf[yh_ * 2, c_, i, z_], colbuf[yh_ * 2 + 1, c_, i, z_]], axis=0
            )
            hi, lo = split(v)
            at = (pl.ds(pl.multiple_of(w * 2 * OWN, 2 * OWN), 2 * OWN), pl.ds(i * 2 * RANK, 2 * RANK))
            rhs_hi[at] = hi
            rhs_lo[at] = lo
        return 0

    lax.fori_loop(0, WIN, column_block, 0)

    half_z = NZ // 2
    for h in range(2):
        at = pl.ds(h * half_z * ROWS, half_z * ROWS)
        part = mm(lhs_hi[at], rhs_hi[...], NT) + (
            mm(lhs_hi[at], rhs_lo[...], NT) + mm(lhs_lo[at], rhs_hi[...], NT)
        )
        pbuf[pl.ds(h * half_z, half_z)] = part.reshape(half_z, ROWS, COLS)

    def partial_to(k):
        return pltpu.make_async_remote_copy(
            pbuf.at[(z + k) % NZ], prec.at[k], g_s.at[k], g_r.at[k], device_id=at_z(k), device_id_type=MESH
        )

    for k in (4, 3, 5, 2, 6, 1, 7):
        partial_to(k).start()
    gram = pbuf[z]
    for k in (1, 7, 2, 6, 3, 5, 4):
        partial_to(k).wait_recv()
        gram = gram + prec[k]
    for t in range(4):
        qsend[t] = gram[:, t * 128 : (t + 1) * 128]

    def block_to(q):
        return pltpu.make_async_remote_copy(
            qsend.at[q // 2], qrecv.at[p], f_s.at[q], f_r.at[p], device_id=dev(p_=q), device_id_type=MESH
        )

    def block_from(q):
        return pltpu.make_async_remote_copy(
            qsend.at[q // 2], qrecv.at[q], f_s.at[q], f_r.at[q], device_id=dev(p_=q), device_id_type=MESH
        )

    for k in (6, 7, 5, 2, 4, 3, 1):
        block_to((p + k) % NP).start()
    qrecv[p] = qsend[p // 2]
    for k in range(1, NP):
        block_from((p + k) % NP).wait_recv()
    shape = (NX * 128, 4 * SEQ)
    lane, col = iota(shape, 0), iota(shape, 1)
    x_, l_ = lane // 128, lane % 128
    goal = ((l_ % 64) // 16) * 64 + ((l_ % 16) // 8) * 32 + x_ * 8 + l_ % 8
    perm = jnp.where((l_ // 64 == p % 2) & (goal == col), 1.0, 0.0).astype(BF16)
    blocks = jnp.concatenate(
        [jnp.concatenate([qrecv[yl_ * NX + i] for i in range(NX)], axis=1) for yl_ in range(2)], axis=0
    )
    hi, rest = blocks.astype(BF16), blocks - blocks.astype(BF16).astype(F32)
    mid, low = split(rest)
    out[...] = mm(hi, perm) + (mm(mid, perm) + mm(low, perm))

    for k in range(1, NP):
        send_part(k).wait_send()
        block_to((p + k) % NP).wait_send()
    for k in range(1, NZ):
        tiles(k).wait_send()
        partial_to(k).wait_send()
    for k in range(1, NX):
        to_x(k).wait_send()
        to_y(k).wait_send()
    for k in range(NY):
        to_core(k).wait_send()


def per_device(acts, grads, positions, proj_in, proj_out, window):
    depth = acts.shape[2]
    vmem, dma = pltpu.VMEM, pltpu.SemaphoreType.DMA
    in_vmem, in_hbm = pl.BlockSpec(memory_space=pltpu.VMEM), pl.BlockSpec(memory_space=pl.ANY)
    tile = (FPZ, NZ, OWN, 2 * RANK)
    scratch = [
        vmem((NP, OWN, LEN, depth), BF16),
        vmem((NP, OWN, LEN, depth), BF16),
        vmem((2, depth, 2 * RANK), BF16),
        vmem((NP, PICK, 2 * RANK), F32),
        vmem((NP, PICK, 2 * RANK), F32),
        vmem((HALF, OWN, 2 * RANK), F32),
        vmem((NX, *tile), F32),
        vmem((NY, NC, *tile), F32),
        vmem((NZ * ROWS, FPZ * 2 * RANK), BF16),
        vmem((NZ * ROWS, FPZ * 2 * RANK), BF16),
        vmem((COLS, FPZ * 2 * RANK), BF16),
        vmem((COLS, FPZ * 2 * RANK), BF16),
        vmem((NZ, ROWS, COLS), F32),
        vmem((NZ, ROWS, COLS), F32),
        vmem((4, ROWS, 128), F32),
        vmem((NP, ROWS, 128), F32),
        dma((2, NP)), dma((1,)),
        dma((NP,)), dma((NP,)), dma((NZ,)), dma((NZ,)), dma((NX,)), dma((NX,)),
        dma((NY,)), dma((NY,)), dma((NY,)), dma((NY,)), dma((NZ,)), dma((NZ,)), dma((NP,)), dma((NP,)),
    ]
    return pl.pallas_call(
        kernel,
        out_shape=jax.ShapeDtypeStruct((SEQ, 4 * SEQ), F32),
        in_specs=[in_hbm, in_hbm, in_vmem, in_vmem, in_vmem, pl.BlockSpec(memory_space=pltpu.SMEM)],
        out_specs=in_vmem,
        scratch_shapes=scratch,
        name="similarity",
        cost_estimate=pl.CostEstimate(flops=1_000_000_000, bytes_accessed=9_000_000, transcendentals=0),
        compiler_params=pltpu.CompilerParams(
            collective_id=0, has_side_effects=True, vmem_limit_bytes=40 << 20
        ),
    )(acts, grads, positions, proj_in, proj_out, window)


def solution(mesh):
    in_specs = (
        P("example", None, "param"),
        P("example", None, "param"),
        P("example", None),
        P("param", None),
        P("param", None),
        P(),
    )
    return jax.shard_map(
        per_device, mesh=mesh, in_specs=in_specs, out_specs=P("example", "param"), check_vma=False
    )
```

```python
import jax
import jax.numpy as jnp
from jax import lax
from jax.experimental import pallas as pl
from jax.experimental.pallas import tpu as pltpu
from jax.sharding import PartitionSpec as P

F32, BF16 = jnp.float32, jnp.bfloat16
MESH = pl.DeviceIdType.MESH
NT = ((1,), (1,))

NP, NX, NY, NZ, NC = 8, 4, 4, 8, 2
SEQ, LEN, LOSS, RANK = 64, 32, 24, 64
LANES = 2 * RANK
OWN = SEQ // NP
WIN = NZ * NY // 2 * NC
TOK = OWN * LEN
PICK = OWN * LOSS
HALF = RANK // 2
FPZ = HALF // NZ
DEEP = FPZ * LANES
ROWS = NX * OWN
PER = 4
SLOT = (0, 1, 7, 2, 6, 3, 5, 4)
PARTS = ((0, 5), (5, 3))
FAR = ((2, 1), (2, 0), (1, 1), (3, 1), (0, 1), (1, 0), (3, 0))


def iota(shape, dim):
    return lax.broadcasted_iota(jnp.int32, shape, dim)


def split(v):
    hi = v.astype(BF16)
    return hi, (v - hi.astype(F32)).astype(BF16)


def mm(a, b, dims=((1,), (0,))):
    return lax.dot_general(a, b, (dims, ((), ())), preferred_element_type=F32)


def kernel(
    acts, grads, pos_hbm, in_hbm, out_hbm, window_hbm, out,
    pos, w_both, xbuf, gbuf, wbuf, hots, sbuf, rbuf, fbuf, rowbuf, colbuf,
    lhs_hi, lhs_lo, rhs_hi, rhs_lo, pbuf, near, fin, window,
    in_sem, loc_sem, a_s, a_r, z_s, z_r, x_s, x_r, y_s, y_r, c_s, c_r, n_s, n_r, f_s, f_r,
):
    p, e = lax.axis_index("param"), lax.axis_index("example")
    yl, x = p // NX, p % NX
    z, yh, c = e // 4, (e // 2) % 2, e % 2
    y = yh * 2 + yl

    def dev(p_, e_):
        return {"param": p_, "example": e_}

    def p_at(dx, dyl):
        return ((yl + dyl) % 2) * NX + (x + dx) % NX

    def e_at(k):
        return ((z + k) % NZ) * 4 + yh * 2 + c

    def at_y(k):
        y_ = (y + k) % NY
        return dev((y_ % 2) * NX + x, z * 4 + (y_ // 2) * 2 + c)

    partner = dev(p, z * 4 + yh * 2 + (1 - c))

    def remote(src, dst, send, recv, to):
        return pltpu.make_async_remote_copy(
            src, dst, send, recv, device_id=to, device_id_type=MESH
        )

    get_factors = [
        pltpu.make_async_copy(pos_hbm, pos, loc_sem.at[2]),
        pltpu.make_async_copy(in_hbm, w_both.at[pl.ds(0, RANK)], loc_sem.at[3]),
        pltpu.make_async_copy(out_hbm, w_both.at[pl.ds(RANK, RANK)], loc_sem.at[4]),
    ]
    for get in get_factors:
        get.start()

    def fetch(q, i):
        src, dst = (acts, xbuf) if i == 0 else (grads, gbuf)
        return pltpu.make_async_copy(
            src.at[pl.ds(pl.multiple_of(q * OWN, OWN), OWN)], dst.at[q], in_sem.at[i, q]
        )

    order = [p_at(*d) for d in FAR] + [p]

    def fetch_next(i):
        if i < NP:
            fetch(order[i], 0).start()
            fetch(order[i], 1).start()

    for i in range(2):
        fetch_next(i)
    get_window = pltpu.make_async_copy(window_hbm, window, loc_sem.at[1])
    get_window.start()

    barrier = pltpu.get_barrier_semaphore()
    others = [dev(p_at(*d), e) for d in FAR]
    for k in (1, 7, 2, 6):
        others += [dev((p + i) % NP, e_at(k)) for i in range(NP)]
    others += [dev(p, e_at(k)) for k in (3, 4, 5)] + [at_y(2), partner]
    others += [dev((1 - yl) * NX + x, z * 4 + (1 - yh) * 2 + c)]
    for d in others:
        pl.semaphore_signal(barrier, inc=1, device_id=d, device_id_type=MESH)

    fetch_next(2)
    pick_t = (iota((PICK, LOSS), 0) % LOSS == iota((PICK, LOSS), 1)).astype(F32).astype(BF16)
    lane = iota((PICK, TOK), 1)
    own_seq = iota((PICK, TOK), 0) // LOSS == lane // LEN
    token = jnp.where(own_seq, lane % LEN, -1).astype(F32)
    spread_at = iota((SEQ, TOK), 0) - iota((SEQ, TOK), 1) // LEN
    get_factors[0].wait()
    pos_t = mm(pick_t, pos[...].astype(F32).astype(BF16)).astype(BF16)
    for i in range(NP):
        spread = (spread_at == order[i] * OWN).astype(F32).astype(BF16)
        hots[i] = (mm(pos_t, spread) == token).astype(F32).astype(BF16)
    for get in get_factors[1:]:
        get.wait()
    both = w_both[...].astype(F32).T
    low = iota(both.shape, 1) < RANK
    wbuf[0] = jnp.where(low, both, 0.0).astype(BF16)
    wbuf[1] = jnp.where(low, 0.0, both).astype(BF16)

    def send_part(i):
        q = p_at(*FAR[i])
        return remote(sbuf.at[i], rbuf.at[i], a_s.at[i], a_r.at[i], dev(q, e))

    def project(i):
        q = order[i]
        fetch(q, 0).wait()
        fetch(q, 1).wait()
        fetch_next(i + 3)
        return mm(xbuf[q].reshape(TOK, -1), wbuf[0]) + mm(gbuf[q].reshape(TOK, -1), wbuf[1])

    def pick(i, ab):
        hi, lo = split(ab)
        return mm(hots[i], hi) + mm(hots[i], lo)

    ab = None
    for i in range(NP):
        ab, before = project(i), ab
        if i > 0:
            sbuf[i - 1] = pick(i - 1, before)
            if i == 1:
                pl.semaphore_wait(barrier, len(others))
            send_part(i - 1).start()
    total = pick(NP - 1, ab)
    for i in range(NP - 1):
        send_part(i).wait_recv()
        total = total + rbuf[i]

    b_t = total.T[RANK:]
    in_seq = iota((OWN, PICK), 1) // LOSS == iota((OWN, PICK), 0)
    a_low = jnp.where(iota((PICK, LANES), 1) < RANK, total, 0.0)
    feats = jnp.zeros((HALF * OWN, LANES), F32)
    for h in range(2):
        b_h = b_t[h * HALF : (h + 1) * HALF]
        b_hi, b_lo = split(jnp.where(in_seq[None], b_h[:, None, :], 0.0).reshape(HALF * OWN, PICK))
        a_hi, a_lo = split(a_low if h == 0 else pltpu.roll(a_low, RANK, 1))
        feats = feats + (mm(b_hi, a_hi) + (mm(b_hi, a_lo) + mm(b_lo, a_hi)))
    fbuf[...] = feats.reshape(HALF, OWN, LANES)

    def tiles(j):
        z_ = (z + SLOT[j]) % NZ
        back = SLOT.index(-SLOT[j] % NZ)
        return remote(
            fbuf.at[pl.ds(z_ * FPZ, FPZ)], rowbuf.at[x, back], z_s.at[j], z_r.at[back], dev(p, e_at(SLOT[j]))
        )

    def tiles_from(j):
        return remote(fbuf.at[pl.ds(0, FPZ)], rowbuf.at[x, j], z_s.at[j], z_r.at[j], dev(p, e_at(SLOT[j])))

    for j in (7, 6, 5, 4, 3, 2, 1):
        tiles(j).start()
    rowbuf[x, 0] = fbuf[pl.ds(z * FPZ, FPZ)]

    def to_x(k, h):
        at = pl.ds(*PARTS[h])
        return remote(
            rowbuf.at[x, at], rowbuf.at[x, at], x_s.at[k, h], x_r.at[k, h], dev(p_at(k, 0), e)
        )

    def from_x(k, h):
        at, x_ = pl.ds(*PARTS[h]), (x + NX - k) % NX
        return remote(
            rowbuf.at[x_, at], rowbuf.at[x_, at], x_s.at[k, h], x_r.at[k, h], dev(p_at(k, 0), e)
        )

    def to_y(k, h):
        at = pl.ds(*PARTS[h])
        return remote(rowbuf.at[x, at], colbuf.at[y, c, at], y_s.at[k, h], y_r.at[k, h], at_y(k))

    def from_y(k, h):
        at, y_ = pl.ds(*PARTS[h]), (y + NY - k) % NY
        return remote(rowbuf.at[x, at], colbuf.at[y_, c, at], y_s.at[k, h], y_r.at[k, h], at_y(k))

    def to_core(k, h):
        at, y_ = pl.ds(*PARTS[h]), (y + NY - k) % NY
        src = rowbuf.at[x, at] if k == 0 else colbuf.at[y_, c, at]
        return remote(src, colbuf.at[y_, c, at], c_s.at[k, h], c_r.at[k, h], partner)

    def from_core(k, h):
        at, y_ = pl.ds(*PARTS[h]), (y + NY - k) % NY
        return remote(rowbuf.at[x, at], colbuf.at[y_, 1 - c, at], c_s.at[k, h], c_r.at[k, h], partner)

    for h, (first, count) in enumerate(PARTS):
        for j in range(max(first, 1), first + count):
            tiles_from(j).wait_recv()
        for k in (1, 3, 2):
            to_y(k, h).start()
            to_x(k, h).start()
        to_core(0, h).start()
    own_cols = pltpu.make_async_copy(rowbuf.at[x], colbuf.at[y, c], loc_sem.at[0])
    own_cols.start()
    for h in range(2):
        for k in (1, 3, 2):
            from_y(k, h).wait_recv()
            to_core(k, h).start()
    for h in range(2):
        for k in (1, 3, 2):
            from_x(k, h).wait_recv()
    for i in range(FPZ):
        rows = jnp.concatenate([rowbuf[:, j, i].reshape(ROWS, LANES) for j in range(NZ)], axis=0)
        hi, lo = split(rows.T)
        lhs_hi[pl.ds(i * LANES, LANES)] = hi
        lhs_lo[pl.ds(i * LANES, LANES)] = lo
    own_cols.wait()
    for h in range(2):
        for k in (0, 1, 3, 2):
            from_core(k, h).wait_recv()
    get_window.wait()

    def columns(g):
        for u in range(2 * PER):
            w = g * 2 * PER + u
            e_ = window[w]
            k = (e_ // 4 + NZ - z) % NZ
            j = jnp.where(k <= 4, jnp.maximum(2 * k - 1, 0), 2 * (NZ - k))
            yh_, c_ = (e_ // 2) % 2, e_ % 2
            for i in range(FPZ):
                v = jnp.concatenate(
                    [colbuf[yh_ * 2, c_, j, i], colbuf[yh_ * 2 + 1, c_, j, i]], axis=0
                )
                hi, lo = split(v)
                at = (pl.ds(u * 2 * OWN, 2 * OWN), pl.ds(i * LANES, LANES))
                rhs_hi[at] = hi
                rhs_lo[at] = lo

    bit = iota((2 * OWN, LANES), 1) // 32

    def swap(a, b, n, shift):
        low = bit // n % 2 == 0
        return jnp.where(low, a, pltpu.roll(b, shift, 1)), jnp.where(low, pltpu.roll(a, LANES - shift, 1), b)

    def products(g):
        hi, lo = rhs_hi[...], rhs_lo[...]
        part = mm(hi, lhs_hi[...]) + (mm(hi, lhs_lo[...]) + mm(lo, lhs_hi[...]))
        for u in range(2):
            for t in range(2):
                one = [
                    part[(u * PER + w) * 2 * OWN : (u * PER + w + 1) * 2 * OWN, t * LANES : (t + 1) * LANES]
                    for w in range(PER)
                ]
                even01, odd01 = swap(one[0], one[1], 1, 32)
                even23, odd23 = swap(one[2], one[3], 1, 32)
                by0, by2 = swap(even01, even23, 2, 64)
                by1, by3 = swap(odd01, odd23, 2, 64)
                for j, by in enumerate((by0, by1, by2, by3)):
                    pbuf[t * 4 + j, g * 2 + u] = by

    groups = [(p // 2 + n) % 4 for n in range(4)]

    def to_near(i, n):
        at = pl.ds(groups[n] * 2, 2)
        if i < 2:
            return remote(
                pbuf.at[5 + i, at], near.at[i, at], n_s.at[i, n], n_r.at[i, n], dev(p, e_at((1, 7)[i]))
            )
        k = jnp.where(groups[n] < 2, 6, 2)
        return remote(pbuf.at[7, at], near.at[2, at], n_s.at[2, n], n_r.at[2, n], dev(p, e_at(k)))

    def block_to(j, n, u):
        back = SLOT.index(-SLOT[j] % NZ)
        p_ = groups[n] * 2 + u
        return remote(pbuf.at[j, p_], fin.at[back, p], f_s.at[j, n, u], f_r.at[back, p], dev(p_, e_at(SLOT[j])))

    def block_from(j, i):
        p_ = (p + NP - i) % NP
        return remote(pbuf.at[j, p_], fin.at[j, p_], f_s.at[0, 0, 0], f_r.at[j, p_], dev(p_, e_at(SLOT[j])))

    def send_blocks(j, n):
        for u in range(2):
            if j == 0 and n == 0:

                @pl.when(p % 2 != u)
                def _():
                    block_to(j, n, u).start()

            else:
                block_to(j, n, u).start()

    for n in range(4):
        columns(groups[n])
        products(groups[n])
        for i in (2, 0, 1):
            to_near(i, n).start()
        for j in (1, 2, 0):
            send_blocks(j, n)
    fin[0, p] = pbuf[0, p]
    for n in range(4):
        for i in range(3):
            to_near(i, n).wait_recv()
        at = pl.ds(groups[n] * 2, 2)
        below = groups[n] < 2
        pbuf[3, at] = pbuf[3, at] + (near[0, at] + jnp.where(below, 0.0, near[2, at]))
        pbuf[4, at] = pbuf[4, at] + (near[1, at] + jnp.where(below, near[2, at], 0.0))
        for j in (3, 4):
            send_blocks(j, n)
    for j in (0, 1, 2, 3, 4):
        for i in range(NP):
            if (j, i) != (0, 0):
                block_from(j, i).wait_recv()
    gram = fin[0]
    for j in range(1, 5):
        gram = gram + fin[j]
    turned = jnp.concatenate(
        [
            gram[yl_ * NX + i, k * OWN : (k + 1) * OWN]
            for yl_ in range(2)
            for k in range(2)
            for i in range(NX)
        ],
        axis=0,
    ).T
    low = iota((ROWS, LANES), 1) < SEQ
    for t in range(2):
        a, b = turned[t * 64 : t * 64 + 32], turned[t * 64 + 32 : t * 64 + 64]
        out[:ROWS, t * LANES : (t + 1) * LANES] = jnp.where(low, a, pltpu.roll(b, SEQ, 1))
        out[ROWS:, t * LANES : (t + 1) * LANES] = jnp.where(low, pltpu.roll(a, SEQ, 1), b)
    for i in range(NP - 1):
        send_part(i).wait_send()
    for j in range(1, NZ):
        tiles(j).wait_send()
    for h in range(2):
        for k in range(1, NX):
            to_x(k, h).wait_send()
            to_y(k, h).wait_send()
        for k in range(NY):
            to_core(k, h).wait_send()
    for n in range(4):
        for i in range(3):
            to_near(i, n).wait_send()
        for j in range(5):
            for u in range(2):
                if j == 0 and n == 0:

                    @pl.when(p % 2 != u)
                    def _():
                        block_to(j, n, u).wait_send()

                else:
                    block_to(j, n, u).wait_send()


def per_device(acts, grads, positions, proj_in, proj_out, window):
    depth = acts.shape[2]
    vmem, dma = pltpu.VMEM, pltpu.SemaphoreType.DMA
    in_vmem, in_hbm = pl.BlockSpec(memory_space=pltpu.VMEM), pl.BlockSpec(memory_space=pltpu.HBM)
    tile = (NZ, FPZ, OWN, LANES)
    scratch = [
        vmem((LOSS, SEQ), jnp.int32),
        vmem((LANES, depth), BF16),
        vmem((NP, OWN, LEN, depth), BF16),
        vmem((NP, OWN, LEN, depth), BF16),
        vmem((2, depth, LANES), BF16),
        vmem((NP, PICK, TOK), BF16),
        vmem((NP - 1, PICK, LANES), F32),
        vmem((NP - 1, PICK, LANES), F32),
        vmem((HALF, OWN, LANES), F32),
        vmem((NX, *tile), F32),
        vmem((NY, NC, *tile), F32),
        vmem((DEEP, NZ * ROWS), BF16),
        vmem((DEEP, NZ * ROWS), BF16),
        vmem((2 * PER * 2 * OWN, DEEP), BF16),
        vmem((2 * PER * 2 * OWN, DEEP), BF16),
        vmem((NZ, NP, 2 * OWN, LANES), F32),
        vmem((3, NP, 2 * OWN, LANES), F32),
        vmem((5, NP, 2 * OWN, LANES), F32),
        pltpu.SMEM((WIN,), jnp.int32),
        dma((2, NP)), dma((5,)),
        dma((NP,)), dma((NP,)), dma((NZ,)), dma((NZ,)), dma((NX, 2)), dma((NX, 2)),
        dma((NY, 2)), dma((NY, 2)), dma((NY, 2)), dma((NY, 2)), dma((3, 4)), dma((3, 4)),
        dma((5, 4, 2)), dma((5, NP)),
    ]
    return pl.pallas_call(
        kernel,
        out_shape=jax.ShapeDtypeStruct((SEQ, 4 * SEQ), F32),
        in_specs=[in_hbm] * 6,
        out_specs=in_vmem,
        scratch_shapes=scratch,
        name="similarity",
        cost_estimate=pl.CostEstimate(flops=1_000_000_000, bytes_accessed=9_000_000, transcendentals=0),
        compiler_params=pltpu.CompilerParams(
            collective_id=0, has_side_effects=True, vmem_limit_bytes=60 << 20
        ),
    )(acts, grads, positions.T, proj_in.T, proj_out.T, window)


def solution(mesh):
    in_specs = (
        P("example", None, "param"),
        P("example", None, "param"),
        P("example", None),
        P("param", None),
        P("param", None),
        P(),
    )
    return jax.shard_map(
        per_device, mesh=mesh, in_specs=in_specs, out_specs=P("example", "param"), check_vma=False
    )
```

```python
import jax
import jax.numpy as jnp
from jax import lax
from jax.experimental import pallas as pl
from jax.experimental.pallas import tpu as pltpu
from jax.sharding import PartitionSpec as P

F32, BF16 = jnp.float32, jnp.bfloat16
MESH = pl.DeviceIdType.MESH
NT = ((1,), (1,))

NP, NX, NY, NZ, NC = 8, 4, 4, 8, 2
SEQ, LEN, LOSS, RANK = 64, 32, 24, 64
LANES = 2 * RANK
OWN = SEQ // NP
WIN = NZ * NY // 2 * NC
TOK = OWN * LEN
PICK = OWN * LOSS
HALF = RANK // 2
FPZ = HALF // NZ
DEEP = FPZ * LANES
ROWS = NX * OWN
PER = 4
GP = 2
NG = NP // GP
SLOT = (0, 1, 7, 2, 6, 3, 5, 4)
PAIRS = NZ // 2
CHUNKS = ((2, 1), (1, 1), (3, 1), (0, 1), (2, 0), (1, 0), (3, 0), (0, 0))
BY_Y = 112
BY_X = PICK - BY_Y


def iota(shape, dim):
    return lax.broadcasted_iota(jnp.int32, shape, dim)


def split(v):
    hi = v.astype(BF16)
    return hi, (v - hi.astype(F32)).astype(BF16)


def mm(a, b, dims=((1,), (0,))):
    return lax.dot_general(a, b, (dims, ((), ())), preferred_element_type=F32)


def kernel(
    acts, grads, pos_hbm, in_hbm, out_hbm, window_hbm, out,
    pos, w_both, xbuf, gbuf, wbuf, hots, sbuf, y_part, x_part, x_sum, y_sum, fbuf, rowbuf, colbuf,
    lhs_hi, lhs_lo, rhs, turned_gram, pbuf, near, fin, window,
    in_sem, loc_sem, a_s, a_r, z_s, z_r, x_s, x_r, y_s, y_r, c_s, c_r, n_s, n_r, f_s, f_r,
):
    p, e = lax.axis_index("param"), lax.axis_index("example")
    yl, x = p // NX, p % NX
    z, yh, c = e // 4, (e // 2) % 2, e % 2
    y = yh * 2 + yl

    def dev(p_, e_):
        return {"param": p_, "example": e_}

    def p_at(dx, dyl):
        return ((yl + dyl) % 2) * NX + (x + dx) % NX

    def e_at(k):
        return ((z + k) % NZ) * 4 + yh * 2 + c

    def at_y(k):
        y_ = (y + k) % NY
        return dev((y_ % 2) * NX + x, z * 4 + (y_ // 2) * 2 + c)

    partner = dev(p, z * 4 + yh * 2 + (1 - c))

    def remote(src, dst, send, recv, to):
        return pltpu.make_async_remote_copy(
            src, dst, send, recv, device_id=to, device_id_type=MESH
        )

    def fetch(q, i):
        src, dst = (acts, xbuf) if i == 0 else (grads, gbuf)
        return pltpu.make_async_copy(
            src.at[pl.ds(pl.multiple_of(q * OWN, OWN), OWN)], dst.at[q], in_sem.at[i, q]
        )

    order = [p_at(*d) for d in CHUNKS]

    def fetch_next(i):
        if i < NP:
            fetch(order[i], 0).start()
            fetch(order[i], 1).start()

    get_factors = [
        pltpu.make_async_copy(pos_hbm, pos, loc_sem.at[2]),
        pltpu.make_async_copy(in_hbm, w_both.at[pl.ds(0, RANK)], loc_sem.at[3]),
        pltpu.make_async_copy(out_hbm, w_both.at[pl.ds(RANK, RANK)], loc_sem.at[4]),
    ]
    for get in get_factors:
        get.start()
    fetch_next(0)
    get_window = pltpu.make_async_copy(window_hbm, window, loc_sem.at[1])
    barrier = pltpu.get_barrier_semaphore()
    others = [dev(p_at(*d), e) for d in CHUNKS[:-1]]
    others += [dev(p, e_at(k)) for k in (3, 4, 5)] + [at_y(2), partner]
    others += [dev((1 - yl) * NX + x, z * 4 + (1 - yh) * 2 + c)]
    for d in others:
        pl.semaphore_signal(barrier, inc=1, device_id=d, device_id_type=MESH)

    def greet(i, _):
        for k in (1, 7, 2, 6):
            pl.semaphore_signal(barrier, inc=1, device_id=dev((p + i) % NP, e_at(k)), device_id_type=MESH)
        return 0

    lax.fori_loop(0, NP, greet, 0)

    fetch_next(1)
    fetch_next(2)
    get_window.start()
    pick_t = (iota((PICK, LOSS), 0) % LOSS == iota((PICK, LOSS), 1)).astype(F32).astype(BF16)
    lane = iota((PICK, TOK), 1)
    own_seq = iota((PICK, TOK), 0) // LOSS == lane // LEN
    token = jnp.where(own_seq, lane % LEN, -1).astype(F32)
    spread_at = iota((SEQ, TOK), 0) - iota((SEQ, TOK), 1) // LEN
    get_factors[0].wait()
    pos_t = mm(pick_t, pos[...].astype(F32).astype(BF16)).astype(BF16)
    for i in range(NP):
        spread = (spread_at == order[i] * OWN).astype(F32).astype(BF16)
        hots[i] = (mm(pos_t, spread) == token).astype(F32).astype(BF16)
    for get in get_factors[1:]:
        get.wait()
    both = w_both[...].astype(F32).T
    low = iota(both.shape, 1) < RANK
    wbuf[0] = jnp.where(low, both, 0.0).astype(BF16)
    wbuf[1] = jnp.where(low, 0.0, both).astype(BF16)

    def to_yl(i):
        dx = CHUNKS[i][0]
        return remote(
            sbuf.at[i, pl.ds(0, BY_Y)], y_part.at[dx], a_s.at[0, dx], a_r.at[0, dx], dev(p_at(0, 1), e)
        )

    def to_own_x(i):
        dx, dyl = CHUNKS[i]
        return remote(
            sbuf.at[i, pl.ds(BY_Y, BY_X)], x_part.at[dyl, dx], a_s.at[1 + dyl, dx], a_r.at[1 + dyl, dx],
            dev(p_at(dx, 0), e),
        )

    def sum_to_x(i):
        dx = CHUNKS[i][0]
        return remote(
            sbuf.at[i, pl.ds(0, BY_Y)], x_sum.at[dx], a_s.at[3, dx], a_r.at[3, dx], dev(p_at(dx, 0), e)
        )

    def sum_to_yl():
        return remote(
            sbuf.at[3, pl.ds(BY_Y, BY_X)], y_sum, a_s.at[3, 0], a_r.at[3, 0], dev(p_at(0, 1), e)
        )

    def send_part(i):
        dx, dyl = CHUNKS[i]
        if dyl:
            to_yl(i).start()
        if dx:
            to_own_x(i).start()

    def project(i):
        q = order[i]
        fetch(q, 0).wait()
        fetch(q, 1).wait()
        fetch_next(i + 3)
        return mm(xbuf[q].reshape(TOK, -1), wbuf[0]) + mm(gbuf[q].reshape(TOK, -1), wbuf[1])

    def pick(i, ab):
        hi, lo = split(ab)
        return mm(hots[i], hi) + mm(hots[i], lo)

    ab = None
    for i in range(NP):
        ab, before = project(i), ab
        if i > 1:
            sbuf[i - 1] = pick(i - 1, before)
            send_part(i - 1)
        if i == 0:
            sbuf[0] = pick(0, ab)
            pl.semaphore_wait(barrier, len(others) + 4 * NP)
            send_part(0)
    own = pick(NP - 1, ab)
    own_y, own_x = own[:BY_Y], own[BY_Y:]
    for i in (4, 5):
        to_yl(i - 4).wait_recv()
        sbuf[i, :BY_Y] = sbuf[i, :BY_Y] + y_part[CHUNKS[i][0]]
        sum_to_x(i).start()
    for i in range(3):
        to_own_x(i).wait_recv()
    sbuf[3, BY_Y:] = sbuf[3, BY_Y:] + (x_part[1, 2] + (x_part[1, 1] + x_part[1, 3]))
    sum_to_yl().start()
    to_yl(2).wait_recv()
    sbuf[6, :BY_Y] = sbuf[6, :BY_Y] + y_part[3]
    sum_to_x(6).start()
    to_yl(3).wait_recv()
    own_y = own_y + y_part[0]
    for i in (4, 5, 6):
        to_own_x(i).wait_recv()
        own_x = own_x + x_part[0, CHUNKS[i][0]]
    for i in (4, 5, 6):
        sum_to_x(i).wait_recv()
        own_y = own_y + x_sum[CHUNKS[i][0]]
    sum_to_yl().wait_recv()
    total = jnp.concatenate([own_y, own_x + y_sum[...]], axis=0)

    b_t = total.T[RANK:]
    in_seq = iota((OWN, PICK), 1) // LOSS == iota((OWN, PICK), 0)
    a_low = jnp.where(iota((PICK, LANES), 1) < RANK, total, 0.0)
    feats = jnp.zeros((HALF * OWN, LANES), F32)
    for h in range(2):
        b_h = b_t[h * HALF : (h + 1) * HALF]
        b_hi, b_lo = split(jnp.where(in_seq[None], b_h[:, None, :], 0.0).reshape(HALF * OWN, PICK))
        a_hi, a_lo = split(a_low if h == 0 else pltpu.roll(a_low, RANK, 1))
        feats = feats + (mm(b_hi, a_hi) + (mm(b_hi, a_lo) + mm(b_lo, a_hi)))
    fbuf[...] = feats.reshape(HALF, OWN, LANES)

    def tiles(j):
        z_ = (z + SLOT[j]) % NZ
        return remote(
            fbuf.at[pl.ds(z_ * FPZ, FPZ)], rowbuf.at[x, z], z_s.at[j], z_r.at[z], dev(p, e_at(SLOT[j]))
        )

    def tiles_from(z_):
        return remote(fbuf.at[pl.ds(0, FPZ)], rowbuf.at[x, z_], z_s.at[0], z_r.at[z_], partner)

    for j in (7, 6, 5, 4, 3, 2, 1):
        tiles(j).start()
    pltpu.make_async_copy(fbuf.at[pl.ds(z * FPZ, FPZ)], rowbuf.at[x, z], z_r.at[z]).start()

    def of_pair(h):
        return pl.ds(pl.multiple_of(pairs[h] * 2, 2), 2)

    step = jnp.where(z % 2 == 0, 3, 1)
    pairs = (z // 2, (z // 2 + step) % 4, (z // 2 + 4 - step) % 4, (z // 2 + 2) % 4)

    def to_x(k, h):
        at = of_pair(h)
        return remote(
            rowbuf.at[x, at], rowbuf.at[x, at], x_s.at[k, h], x_r.at[k, h], dev(p_at(k, 0), e)
        )

    def from_x(k, h):
        at, x_ = of_pair(h), (x + NX - k) % NX
        return remote(
            rowbuf.at[x_, at], rowbuf.at[x_, at], x_s.at[k, h], x_r.at[k, h], dev(p_at(k, 0), e)
        )

    def to_y(k, h):
        at = of_pair(h)
        return remote(rowbuf.at[x, at], colbuf.at[y, c, at], y_s.at[k, h], y_r.at[k, h], at_y(k))

    def from_y(k, h):
        at, y_ = of_pair(h), (y + NY - k) % NY
        return remote(rowbuf.at[x, at], colbuf.at[y_, c, at], y_s.at[k, h], y_r.at[k, h], at_y(k))

    def to_core(k, h):
        at, y_ = of_pair(h), (y + NY - k) % NY
        src = rowbuf.at[x, at] if k == 0 else colbuf.at[y_, c, at]
        return remote(src, colbuf.at[y_, c, at], c_s.at[k, h], c_r.at[k, h], partner)

    def from_core(k, h):
        at, y_ = of_pair(h), (y + NY - k) % NY
        return remote(rowbuf.at[x, at], colbuf.at[y_, 1 - c, at], c_s.at[k, h], c_r.at[k, h], partner)

    for h in range(PAIRS):
        for u in range(2):
            tiles_from(pairs[h] * 2 + u).wait_recv()
        for k in (1, 3, 2):
            to_y(k, h).start()
            to_x(k, h).start()
        to_core(0, h).start()
    own_cols = pltpu.make_async_copy(rowbuf.at[x], colbuf.at[y, c], loc_sem.at[0])
    own_cols.start()
    for h in range(PAIRS):
        for k in (1, 3, 2):
            from_y(k, h).wait_recv()
            to_core(k, h).start()
    for h in range(PAIRS):
        for k in (1, 3, 2):
            from_x(k, h).wait_recv()
    for i in range(FPZ):
        rows = jnp.concatenate([rowbuf[:, (z + SLOT[j]) % NZ, i].reshape(ROWS, LANES) for j in range(NZ)], axis=0)
        hi, lo = split(rows.T)
        lhs_hi[pl.ds(i * LANES, LANES)] = hi
        lhs_lo[pl.ds(i * LANES, LANES)] = lo
    def products(c_, yhs):
        n = len(yhs) * NZ * 2 * OWN

        def columns(z_, _):
            for k, yh_ in enumerate(yhs):
                at = pl.multiple_of((k * NZ + z_) * 2 * OWN, 2 * OWN)
                for i in range(FPZ):
                    v = jnp.concatenate([colbuf[yh_ * 2, c_, z_, i], colbuf[yh_ * 2 + 1, c_, z_, i]], axis=0)
                    hi, lo = split(v)
                    rhs[pl.ds(at, 2 * OWN), i * LANES : (i + 1) * LANES] = hi
                    rhs[pl.ds(n + at, 2 * OWN), i * LANES : (i + 1) * LANES] = lo
            return 0

        lax.fori_loop(0, NZ, columns, 0)
        both = mm(rhs[: 2 * n], lhs_hi[...])
        part = both[:n] + (both[n:] + mm(rhs[:n], lhs_lo[...]))
        for k, yh_ in enumerate(yhs):
            rows = part[k * NZ * 2 * OWN : (k + 1) * NZ * 2 * OWN]
            turned_gram[c_, yh_] = rows.reshape(NZ, 2 * OWN, NZ * ROWS)

    own_cols.wait()
    products(c, (0, 1))
    beside = jnp.where(yl == 0, 3, 1)
    for h in range(PAIRS):
        from_core(0, h).wait_recv()
        from_core(beside, h).wait_recv()
    products(1 - c, (yh,))
    for h in range(PAIRS):
        from_core(4 - beside, h).wait_recv()
        from_core(2, h).wait_recv()
    products(1 - c, (1 - yh,))
    get_window.wait()

    bit = iota((2 * OWN, LANES), 1) // 32

    def swap(a, b, n, shift):
        low = bit // n % 2 == 0
        return jnp.where(low, a, pltpu.roll(b, shift, 1)), jnp.where(low, pltpu.roll(a, LANES - shift, 1), b)

    def pack(g):
        for u in range(GP):
            es = [window[(g * GP + u) * PER + w] for w in range(PER)]
            for t in range(2):
                one = [
                    turned_gram[e_ % 2, (e_ // 2) % 2, e_ // 4, :, t * LANES : (t + 1) * LANES] for e_ in es
                ]
                even01, odd01 = swap(one[0], one[1], 1, 32)
                even23, odd23 = swap(one[2], one[3], 1, 32)
                by0, by2 = swap(even01, even23, 2, 64)
                by1, by3 = swap(odd01, odd23, 2, 64)
                for j, by in enumerate((by0, by1, by2, by3)):
                    pbuf[t * 4 + j, g * GP + u] = by

    def group(n):
        return (p // GP + n) % NG

    def to_near(i, n):
        at = pl.ds(group(n) * GP, GP)
        if i < 2:
            return remote(
                pbuf.at[5 + i, at], near.at[i, at], n_s.at[i, n], n_r.at[i, n], dev(p, e_at((1, 7)[i]))
            )
        k = jnp.where(group(n) < NG // 2, 6, 2)
        return remote(pbuf.at[7, at], near.at[2, at], n_s.at[2, n], n_r.at[2, n], dev(p, e_at(k)))

    def block_to(j, n, u):
        back = SLOT.index(-SLOT[j] % NZ)
        p_ = group(n) * GP + u
        return remote(pbuf.at[j, p_], fin.at[back, p], f_s.at[j, n, u], f_r.at[back, p], dev(p_, e_at(SLOT[j])))

    def block_from(j, i):
        p_ = (p + NP - i) % NP
        return remote(pbuf.at[j, p_], fin.at[j, p_], f_s.at[0, 0, 0], f_r.at[j, p_], dev(p_, e_at(SLOT[j])))

    def send_blocks(n, js):
        for u in range(GP):
            for j in js:
                if j:
                    block_to(j, n, u).start()
                else:

                    @pl.when(group(n) * GP + u != p)
                    def _():
                        block_to(j, n, u).start()

    def far_rows(n, _):
        pack(group(n))
        for i in (2, 0, 1):
            to_near(i, n).start()
        return 0

    def near_rows(n, _):
        send_blocks(n, (1, 2, 0))
        return 0

    def merge(n, _):
        for i in range(3):
            to_near(i, n).wait_recv()
        at = pl.ds(group(n) * GP, GP)
        below = group(n) < NG // 2
        pbuf[3, at] = pbuf[3, at] + (near[0, at] + jnp.where(below, 0.0, near[2, at]))
        pbuf[4, at] = pbuf[4, at] + (near[1, at] + jnp.where(below, near[2, at], 0.0))
        send_blocks(n, (3, 4))
        return 0

    lax.fori_loop(0, NG, far_rows, 0)
    lax.fori_loop(0, NG, near_rows, 0)
    fin[0, p] = pbuf[0, p]
    lax.fori_loop(0, NG, merge, 0)
    def arrived(i, _):
        for j in range(5):
            if j:
                block_from(j, i).wait_recv()
            else:

                @pl.when(i != 0)
                def _():
                    block_from(0, i).wait_recv()

        return 0

    lax.fori_loop(0, NP, arrived, 0)
    gram = fin[0]
    for j in range(1, 5):
        gram = gram + fin[j]
    turned = jnp.concatenate(
        [
            gram[yl_ * NX + i, k * OWN : (k + 1) * OWN]
            for yl_ in range(2)
            for k in range(2)
            for i in range(NX)
        ],
        axis=0,
    ).T
    low = iota((ROWS, LANES), 1) < SEQ
    for t in range(2):
        a, b = turned[t * 64 : t * 64 + 32], turned[t * 64 + 32 : t * 64 + 64]
        out[:ROWS, t * LANES : (t + 1) * LANES] = jnp.where(low, a, pltpu.roll(b, SEQ, 1))
        out[ROWS:, t * LANES : (t + 1) * LANES] = jnp.where(low, pltpu.roll(a, SEQ, 1), b)
    for i, (dx, dyl) in enumerate(CHUNKS):
        if dyl:
            to_yl(i).wait_send()
        if dx:
            to_own_x(i).wait_send()
        if dx and not dyl:
            sum_to_x(i).wait_send()
    sum_to_yl().wait_send()
    for j in range(1, NZ):
        tiles(j).wait_send()
    for h in range(PAIRS):
        for k in range(1, NX):
            to_x(k, h).wait_send()
            to_y(k, h).wait_send()
        for k in range(NY):
            to_core(k, h).wait_send()
    def sent(n, _):
        for i in range(3):
            to_near(i, n).wait_send()
        for u in range(GP):
            for j in range(5):
                if j:
                    block_to(j, n, u).wait_send()
                else:

                    @pl.when(group(n) * GP + u != p)
                    def _():
                        block_to(j, n, u).wait_send()

        return 0

    lax.fori_loop(0, NG, sent, 0)


def per_device(acts, grads, positions, proj_in, proj_out, window):
    depth = acts.shape[2]
    vmem, dma = pltpu.VMEM, pltpu.SemaphoreType.DMA
    in_vmem, in_hbm = pl.BlockSpec(memory_space=pltpu.VMEM), pl.BlockSpec(memory_space=pltpu.HBM)
    tile = (NZ, FPZ, OWN, LANES)
    scratch = [
        vmem((LOSS, SEQ), jnp.int32),
        vmem((LANES, depth), BF16),
        vmem((NP, OWN, LEN, depth), BF16),
        vmem((NP, OWN, LEN, depth), BF16),
        vmem((2, depth, LANES), BF16),
        vmem((NP, PICK, TOK), BF16),
        vmem((NP - 1, PICK, LANES), F32),
        vmem((NX, BY_Y, LANES), F32),
        vmem((2, NX, BY_X, LANES), F32),
        vmem((NX, BY_Y, LANES), F32),
        vmem((BY_X, LANES), F32),
        vmem((HALF, OWN, LANES), F32),
        vmem((NX, *tile), F32),
        vmem((NY, NC, *tile), F32),
        vmem((DEEP, NZ * ROWS), BF16),
        vmem((DEEP, NZ * ROWS), BF16),
        vmem((4 * NZ * 2 * OWN, DEEP), BF16),
        vmem((NC, 2, NZ, 2 * OWN, NZ * ROWS), F32),
        vmem((NZ, NP, 2 * OWN, LANES), F32),
        vmem((3, NP, 2 * OWN, LANES), F32),
        vmem((5, NP, 2 * OWN, LANES), F32),
        pltpu.SMEM((WIN,), jnp.int32),
        dma((2, NP)), dma((5,)),
        dma((4, NX)), dma((4, NX)), dma((NZ,)), dma((NZ,)), dma((NX, PAIRS)), dma((NX, PAIRS)),
        dma((NY, PAIRS)), dma((NY, PAIRS)), dma((NY, PAIRS)), dma((NY, PAIRS)), dma((3, NG)), dma((3, NG)),
        dma((5, NG, GP)), dma((5, NP)),
    ]
    return pl.pallas_call(
        kernel,
        out_shape=jax.ShapeDtypeStruct((SEQ, 4 * SEQ), F32),
        in_specs=[in_hbm] * 6,
        out_specs=in_vmem,
        scratch_shapes=scratch,
        name="similarity",
        cost_estimate=pl.CostEstimate(flops=1_000_000_000, bytes_accessed=9_000_000, transcendentals=0),
        compiler_params=pltpu.CompilerParams(
            collective_id=0, has_side_effects=True, vmem_limit_bytes=60 << 20
        ),
    )(acts, grads, positions.T, proj_in.T, proj_out.T, window)


def solution(mesh):
    in_specs = (
        P("example", None, "param"),
        P("example", None, "param"),
        P("example", None),
        P("param", None),
        P("param", None),
        P(),
    )
    return jax.shard_map(
        per_device, mesh=mesh, in_specs=in_specs, out_specs=P("example", "param"), check_vma=False
    )
```

```python
import jax
import jax.numpy as jnp
from jax import lax
from jax.experimental import pallas as pl
from jax.experimental.pallas import tpu as pltpu
from jax.sharding import PartitionSpec as P

F32, BF16 = jnp.float32, jnp.bfloat16
MESH = pl.DeviceIdType.MESH
NT = ((1,), (1,))

NP, NX, NY, NZ, NC = 8, 4, 4, 8, 2
SEQ, LEN, LOSS, RANK = 64, 32, 24, 64
LANES = 2 * RANK
OWN = SEQ // NP
WIN = NZ * NY // 2 * NC
TOK = OWN * LEN
PICK = OWN * LOSS
HALF = RANK // 2
FPZ = HALF // NZ
DEEP = FPZ * LANES
ROWS = NX * OWN
PER = 4
GP = 2
NG = NP // GP
SLOT = (0, 1, 7, 2, 6, 3, 5, 4)
PAIRS = NZ // 2
CHUNKS = ((2, 1), (1, 1), (3, 1), (0, 1), (2, 0), (1, 0), (3, 0), (0, 0))
BY_Y = 112
BY_X = PICK - BY_Y


def iota(shape, dim):
    return lax.broadcasted_iota(jnp.int32, shape, dim)


def split(v):
    hi = v.astype(BF16)
    return hi, (v - hi.astype(F32)).astype(BF16)


def mm(a, b, dims=((1,), (0,))):
    return lax.dot_general(a, b, (dims, ((), ())), preferred_element_type=F32)


def kernel(
    acts, grads, pos_hbm, in_hbm, out_hbm, window_hbm, out,
    pos, w_both, tokens, wbuf, hots, sbuf, y_part, x_part, x_sum, y_sum, fbuf, rowbuf, colbuf,
    lhs_hi, lhs_lo, rhs, turned_gram, pbuf, near, fin, window,
    in_sem, loc_sem, a_s, a_r, z_s, z_r, x_s, x_r, y_s, y_r, c_s, c_r, n_s, n_r, f_s, f_r,
):
    p, e = lax.axis_index("param"), lax.axis_index("example")
    yl, x = p // NX, p % NX
    z, yh, c = e // 4, (e // 2) % 2, e % 2
    y = yh * 2 + yl

    def dev(p_, e_):
        return {"param": p_, "example": e_}

    def p_at(dx, dyl):
        return ((yl + dyl) % 2) * NX + (x + dx) % NX

    def e_at(k):
        return ((z + k) % NZ) * 4 + yh * 2 + c

    def at_y(k):
        y_ = (y + k) % NY
        return dev((y_ % 2) * NX + x, z * 4 + (y_ // 2) * 2 + c)

    partner = dev(p, z * 4 + yh * 2 + (1 - c))

    def remote(src, dst, send, recv, to):
        return pltpu.make_async_remote_copy(
            src, dst, send, recv, device_id=to, device_id_type=MESH
        )

    def all_arrived(ref, sem):
        remote(ref, ref, sem, sem, partner).wait_recv()

    def all_sent(ref, sem):
        remote(ref, ref, sem, sem, partner).wait_send()

    order = [p_at(*d) for d in CHUNKS]

    def fetch_next(i):
        if i < NP:
            at = pl.ds(pl.multiple_of(order[i] * OWN, OWN), OWN)
            for k, src in enumerate((acts, grads)):
                pltpu.make_async_copy(src.at[at], tokens.at[i, k], in_sem.at[i % 3]).start()

    get_factors = [
        pltpu.make_async_copy(pos_hbm, pos, loc_sem.at[2]),
        pltpu.make_async_copy(in_hbm, w_both.at[pl.ds(0, RANK)], loc_sem.at[3]),
        pltpu.make_async_copy(out_hbm, w_both.at[pl.ds(RANK, RANK)], loc_sem.at[3]),
    ]
    for get in get_factors:
        get.start()
    fetch_next(0)
    get_window = pltpu.make_async_copy(window_hbm, window, loc_sem.at[1])
    barrier = pltpu.get_barrier_semaphore()
    others = [dev(p_at(*d), e) for d in CHUNKS[:-1]]
    others += [dev(p, e_at(k)) for k in (3, 4, 5)] + [at_y(2), partner]
    others += [dev((1 - yl) * NX + x, z * 4 + (1 - yh) * 2 + c)]
    for d in others:
        pl.semaphore_signal(barrier, inc=1, device_id=d, device_id_type=MESH)

    def greet(i, _):
        for k in (1, 7, 2, 6):
            pl.semaphore_signal(barrier, inc=1, device_id=dev((p + i) % NP, e_at(k)), device_id_type=MESH)
        return 0

    lax.fori_loop(0, NP, greet, 0)

    fetch_next(1)
    fetch_next(2)
    get_window.start()
    pick_t = (iota((PICK, LOSS), 0) % LOSS == iota((PICK, LOSS), 1)).astype(F32).astype(BF16)
    lane = iota((PICK, TOK), 1)
    own_seq = iota((PICK, TOK), 0) // LOSS == lane // LEN
    token = jnp.where(own_seq, lane % LEN, -1).astype(F32)
    spread_at = iota((SEQ, TOK), 0) - iota((SEQ, TOK), 1) // LEN
    get_factors[0].wait()
    pos_t = mm(pick_t, pos[...].astype(F32).astype(BF16)).astype(BF16)
    for i in range(NP):
        spread = (spread_at == order[i] * OWN).astype(F32).astype(BF16)
        hots[i] = (mm(pos_t, spread) == token).astype(F32).astype(BF16)
    pltpu.make_async_copy(w_both, w_both, loc_sem.at[3]).wait()
    both = w_both[...].astype(F32).T
    low = iota(both.shape, 1) < RANK
    wbuf[0] = jnp.where(low, both, 0.0).astype(BF16)
    wbuf[1] = jnp.where(low, 0.0, both).astype(BF16)

    def to_yl(i):
        dx = CHUNKS[i][0]
        return remote(
            sbuf.at[i, pl.ds(0, BY_Y)], y_part.at[dx], a_s.at[0], a_r.at[dx], dev(p_at(0, 1), e)
        )

    def to_own_x(i):
        dx, dyl = CHUNKS[i]
        return remote(
            sbuf.at[i, pl.ds(BY_Y, BY_X)], x_part.at[dyl, dx], a_s.at[0], a_r.at[4 + dyl],
            dev(p_at(dx, 0), e),
        )

    def sum_to_x(i):
        dx = CHUNKS[i][0]
        return remote(
            sbuf.at[i, pl.ds(0, BY_Y)], x_sum.at[dx], a_s.at[0], a_r.at[6], dev(p_at(dx, 0), e)
        )

    def sum_to_yl():
        return remote(
            sbuf.at[3, pl.ds(BY_Y, BY_X)], y_sum, a_s.at[0], a_r.at[7], dev(p_at(0, 1), e)
        )

    def send_part(i):
        dx, dyl = CHUNKS[i]
        if dyl:
            to_yl(i).start()
        if dx:
            to_own_x(i).start()

    def project(i):
        pltpu.make_async_copy(tokens.at[i], tokens.at[i], in_sem.at[i % 3]).wait()
        fetch_next(i + 3)
        return mm(tokens[i, 0].reshape(TOK, -1), wbuf[0]) + mm(tokens[i, 1].reshape(TOK, -1), wbuf[1])

    def pick(i, ab):
        hi, lo = split(ab)
        return mm(hots[i], hi) + mm(hots[i], lo)

    ab = None
    for i in range(NP):
        ab, before = project(i), ab
        if i > 1:
            sbuf[i - 1] = pick(i - 1, before)
            send_part(i - 1)
        if i == 0:
            sbuf[0] = pick(0, ab)
            pl.semaphore_wait(barrier, len(others) + 4 * NP)
            send_part(0)
    own = pick(NP - 1, ab)
    own_y, own_x = own[:BY_Y], own[BY_Y:]
    for i in (4, 5):
        to_yl(i - 4).wait_recv()
        sbuf[i, :BY_Y] = sbuf[i, :BY_Y] + y_part[CHUNKS[i][0]]
        sum_to_x(i).start()
    all_arrived(x_part.at[1, pl.ds(1, 3)], a_r.at[5])
    sbuf[3, BY_Y:] = sbuf[3, BY_Y:] + (x_part[1, 2] + (x_part[1, 1] + x_part[1, 3]))
    sum_to_yl().start()
    to_yl(2).wait_recv()
    sbuf[6, :BY_Y] = sbuf[6, :BY_Y] + y_part[3]
    sum_to_x(6).start()
    to_yl(3).wait_recv()
    own_y = own_y + y_part[0]
    all_arrived(x_part.at[0, pl.ds(1, 3)], a_r.at[4])
    own_x = own_x + (x_part[0, 2] + (x_part[0, 1] + x_part[0, 3]))
    all_arrived(x_sum.at[pl.ds(1, 3)], a_r.at[6])
    own_y = own_y + (x_sum[2] + (x_sum[1] + x_sum[3]))
    sum_to_yl().wait_recv()
    total = jnp.concatenate([own_y, own_x + y_sum[...]], axis=0)

    b_t = total.T[RANK:]
    in_seq = iota((OWN, PICK), 1) // LOSS == iota((OWN, PICK), 0)
    a_low = jnp.where(iota((PICK, LANES), 1) < RANK, total, 0.0)
    feats = jnp.zeros((HALF * OWN, LANES), F32)
    for h in range(2):
        b_h = b_t[h * HALF : (h + 1) * HALF]
        b_hi, b_lo = split(jnp.where(in_seq[None], b_h[:, None, :], 0.0).reshape(HALF * OWN, PICK))
        a_hi, a_lo = split(a_low if h == 0 else pltpu.roll(a_low, RANK, 1))
        feats = feats + (mm(b_hi, a_hi) + (mm(b_hi, a_lo) + mm(b_lo, a_hi)))
    fbuf[...] = feats.reshape(HALF, OWN, LANES)

    def tiles(j):
        z_ = (z + SLOT[j]) % NZ
        return remote(
            fbuf.at[pl.ds(z_ * FPZ, FPZ)], rowbuf.at[x, z], z_s.at[0], z_r.at[z // 2], dev(p, e_at(SLOT[j]))
        )

    for j in (7, 6, 5, 4, 3, 2, 1):
        tiles(j).start()
    pltpu.make_async_copy(fbuf.at[pl.ds(z * FPZ, FPZ)], rowbuf.at[x, z], z_r.at[z // 2]).start()

    def of_pair(h):
        return pl.ds(pl.multiple_of(pairs[h] * 2, 2), 2)

    step = jnp.where(z % 2 == 0, 3, 1)
    pairs = (z // 2, (z // 2 + step) % 4, (z // 2 + 4 - step) % 4, (z // 2 + 2) % 4)

    def to_x(k, h):
        at = of_pair(h)
        return remote(
            rowbuf.at[x, at], rowbuf.at[x, at], x_s.at[0], x_r.at[0], dev(p_at(k, 0), e)
        )

    def to_y(k, h):
        at = of_pair(h)
        return remote(rowbuf.at[x, at], colbuf.at[y, c, at], y_s.at[0], y_r.at[k, h], at_y(k))

    def from_y(k, h):
        at, y_ = of_pair(h), (y + NY - k) % NY
        return remote(rowbuf.at[x, at], colbuf.at[y_, c, at], y_s.at[0], y_r.at[k, h], at_y(k))

    def to_core(k, h):
        at, y_ = of_pair(h), (y + NY - k) % NY
        src = rowbuf.at[x, at] if k == 0 else colbuf.at[y_, c, at]
        return remote(src, colbuf.at[y_, c, at], c_s.at[0], c_r.at[(y_ // 2 + yh) % 2], partner)

    for h in range(PAIRS):
        all_arrived(rowbuf.at[x, of_pair(h)], z_r.at[pairs[h]])
        for k in (1, 3, 2):
            to_y(k, h).start()
            to_x(k, h).start()
        to_core(0, h).start()
    own_cols = pltpu.make_async_copy(rowbuf.at[x], colbuf.at[y, c], loc_sem.at[0])
    own_cols.start()
    for h in range(PAIRS):
        for k in (1, 3, 2):
            from_y(k, h).wait_recv()
            to_core(k, h).start()
    all_arrived(rowbuf.at[pl.ds(0, 3)], x_r.at[0])
    for i in range(FPZ):
        rows = jnp.concatenate([rowbuf[:, (z + SLOT[j]) % NZ, i].reshape(ROWS, LANES) for j in range(NZ)], axis=0)
        hi, lo = split(rows.T)
        lhs_hi[pl.ds(i * LANES, LANES)] = hi
        lhs_lo[pl.ds(i * LANES, LANES)] = lo
    def products(c_, yhs):
        n = len(yhs) * NZ * 2 * OWN

        def columns(z_, _):
            for k, yh_ in enumerate(yhs):
                at = pl.multiple_of((k * NZ + z_) * 2 * OWN, 2 * OWN)
                for i in range(FPZ):
                    v = jnp.concatenate([colbuf[yh_ * 2, c_, z_, i], colbuf[yh_ * 2 + 1, c_, z_, i]], axis=0)
                    hi, lo = split(v)
                    rhs[pl.ds(at, 2 * OWN), i * LANES : (i + 1) * LANES] = hi
                    rhs[pl.ds(n + at, 2 * OWN), i * LANES : (i + 1) * LANES] = lo
            return 0

        lax.fori_loop(0, NZ, columns, 0)
        both = mm(rhs[: 2 * n], lhs_hi[...])
        part = both[:n] + (both[n:] + mm(rhs[:n], lhs_lo[...]))
        for k, yh_ in enumerate(yhs):
            rows = part[k * NZ * 2 * OWN : (k + 1) * NZ * 2 * OWN]
            turned_gram[c_, yh_] = rows.reshape(NZ, 2 * OWN, NZ * ROWS)

    own_cols.wait()
    products(c, (0, 1))
    all_arrived(colbuf.at[pl.ds(0, 2), 0], c_r.at[0])
    products(1 - c, (yh,))
    all_arrived(colbuf.at[pl.ds(0, 2), 0], c_r.at[1])
    products(1 - c, (1 - yh,))
    get_window.wait()

    bit = iota((2 * OWN, LANES), 1) // 32

    def swap(a, b, n, shift):
        low = bit // n % 2 == 0
        return jnp.where(low, a, pltpu.roll(b, shift, 1)), jnp.where(low, pltpu.roll(a, LANES - shift, 1), b)

    def pack(g):
        for u in range(GP):
            es = [window[(g * GP + u) * PER + w] for w in range(PER)]
            for t in range(2):
                one = [
                    turned_gram[e_ % 2, (e_ // 2) % 2, e_ // 4, :, t * LANES : (t + 1) * LANES] for e_ in es
                ]
                even01, odd01 = swap(one[0], one[1], 1, 32)
                even23, odd23 = swap(one[2], one[3], 1, 32)
                by0, by2 = swap(even01, even23, 2, 64)
                by1, by3 = swap(odd01, odd23, 2, 64)
                for j, by in enumerate((by0, by1, by2, by3)):
                    pbuf[t * 4 + j, g * GP + u] = by

    def group(n):
        return (p // GP + n) % NG

    def to_near(i, n):
        at = pl.ds(group(n) * GP, GP)
        if i < 2:
            return remote(
                pbuf.at[5 + i, at], near.at[i, at], n_s.at[0], n_r.at[n], dev(p, e_at((1, 7)[i]))
            )
        k = jnp.where(group(n) < NG // 2, 6, 2)
        return remote(pbuf.at[7, at], near.at[2, at], n_s.at[0], n_r.at[n], dev(p, e_at(k)))

    def block_to(j, n, u):
        back = SLOT.index(-SLOT[j] % NZ)
        p_ = group(n) * GP + u
        at = back * NP + (p_ + NP - p) % NP
        return remote(pbuf.at[j, p_], fin.at[at], f_s.at[0], f_r.at[0], dev(p_, e_at(SLOT[j])))

    def send_blocks(n, js):
        for u in range(GP):
            for j in js:
                if j:
                    block_to(j, n, u).start()
                else:

                    @pl.when(group(n) * GP + u != p)
                    def _():
                        block_to(j, n, u).start()

    def far_rows(n, _):
        pack(group(n))
        for i in (2, 0, 1):
            to_near(i, n).start()
        return 0

    def near_rows(n, _):
        send_blocks(n, (1, 2, 0))
        return 0

    def merge(n, _):
        at = pl.ds(group(n) * GP, GP)
        all_arrived(near.at[:, at], n_r.at[n])
        below = group(n) < NG // 2
        pbuf[3, at] = pbuf[3, at] + (near[0, at] + jnp.where(below, 0.0, near[2, at]))
        pbuf[4, at] = pbuf[4, at] + (near[1, at] + jnp.where(below, near[2, at], 0.0))
        send_blocks(n, (3, 4))
        return 0

    lax.fori_loop(0, NG, far_rows, 0)
    lax.fori_loop(0, NG, near_rows, 0)
    fin[0] = pbuf[0, p]
    lax.fori_loop(0, NG, merge, 0)
    all_arrived(fin.at[pl.ds(1, 5 * NP - 1)], f_r.at[0])

    def gram_from(p_):
        i = (p + NP - p_) % NP
        return (fin[i] + (fin[NP + i] + fin[2 * NP + i])) + (fin[3 * NP + i] + fin[4 * NP + i])

    gram = [gram_from(p_) for p_ in range(NP)]
    turned = jnp.concatenate(
        [
            gram[yl_ * NX + i][k * OWN : (k + 1) * OWN]
            for yl_ in range(2)
            for k in range(2)
            for i in range(NX)
        ],
        axis=0,
    ).T
    low = iota((ROWS, LANES), 1) < SEQ
    for t in range(2):
        a, b = turned[t * 64 : t * 64 + 32], turned[t * 64 + 32 : t * 64 + 64]
        out[:ROWS, t * LANES : (t + 1) * LANES] = jnp.where(low, a, pltpu.roll(b, SEQ, 1))
        out[ROWS:, t * LANES : (t + 1) * LANES] = jnp.where(low, pltpu.roll(a, SEQ, 1), b)
    all_sent(sbuf, a_s.at[0])
    all_sent(rowbuf.at[0, pl.ds(0, NZ - 1)], z_s.at[0])
    all_sent(rowbuf.at[pl.ds(0, 3)], x_s.at[0])
    all_sent(rowbuf.at[pl.ds(0, 3)], y_s.at[0])
    all_sent(rowbuf, c_s.at[0])
    all_sent(near, n_s.at[0])
    all_sent(fin.at[pl.ds(1, 5 * NP - 1)], f_s.at[0])


def per_device(acts, grads, positions, proj_in, proj_out, window):
    depth = acts.shape[2]
    vmem, dma = pltpu.VMEM, pltpu.SemaphoreType.DMA
    in_vmem, in_hbm = pl.BlockSpec(memory_space=pltpu.VMEM), pl.BlockSpec(memory_space=pltpu.HBM)
    tile = (NZ, FPZ, OWN, LANES)
    scratch = [
        vmem((LOSS, SEQ), jnp.int32),
        vmem((LANES, depth), BF16),
        vmem((NP, 2, OWN, LEN, depth), BF16),
        vmem((2, depth, LANES), BF16),
        vmem((NP, PICK, TOK), BF16),
        vmem((NP - 1, PICK, LANES), F32),
        vmem((NX, BY_Y, LANES), F32),
        vmem((2, NX, BY_X, LANES), F32),
        vmem((NX, BY_Y, LANES), F32),
        vmem((BY_X, LANES), F32),
        vmem((HALF, OWN, LANES), F32),
        vmem((NX, *tile), F32),
        vmem((NY, NC, *tile), F32),
        vmem((DEEP, NZ * ROWS), BF16),
        vmem((DEEP, NZ * ROWS), BF16),
        vmem((4 * NZ * 2 * OWN, DEEP), BF16),
        vmem((NC, 2, NZ, 2 * OWN, NZ * ROWS), F32),
        vmem((NZ, NP, 2 * OWN, LANES), F32),
        vmem((3, NP, 2 * OWN, LANES), F32),
        vmem((5 * NP, 2 * OWN, LANES), F32),
        pltpu.SMEM((WIN,), jnp.int32),
        dma((3,)), dma((4,)),
        dma((1,)), dma((8,)), dma((1,)), dma((4,)), dma((1,)), dma((1,)),
        dma((1,)), dma((NY, PAIRS)), dma((1,)), dma((2,)), dma((1,)), dma((NG,)),
        dma((1,)), dma((1,)),
    ]
    operands = (acts, grads, positions.T, proj_in.T, proj_out.T, window)
    return pl.pallas_call(
        kernel,
        out_shape=jax.ShapeDtypeStruct((SEQ, 4 * SEQ), F32),
        in_specs=[in_hbm] * 6,
        out_specs=in_vmem,
        scratch_shapes=scratch,
        name="similarity",
        cost_estimate=pl.CostEstimate(flops=1_000_000_000, bytes_accessed=9_000_000, transcendentals=0),
        compiler_params=pltpu.CompilerParams(
            collective_id=0, has_side_effects=True, vmem_limit_bytes=40 << 20
        ),
    )(*(pltpu.with_memory_space_constraint(v, pltpu.HBM) for v in operands))


def solution(mesh):
    in_specs = (
        P("example", None, "param"),
        P("example", None, "param"),
        P("example", None),
        P("param", None),
        P("param", None),
        P(),
    )
    return jax.shard_map(
        per_device, mesh=mesh, in_specs=in_specs, out_specs=P("example", "param"), check_vma=False
    )
```

```python
import jax
import jax.numpy as jnp
from jax import lax
from jax.experimental import pallas as pl
from jax.experimental.pallas import tpu as pltpu
from jax.sharding import PartitionSpec as P

F32, BF16 = jnp.float32, jnp.bfloat16
MESH = pl.DeviceIdType.MESH
NT = ((1,), (1,))

NP, NX, NY, NZ, NC = 8, 4, 4, 8, 2
SEQ, LEN, LOSS, RANK = 64, 32, 24, 64
LANES = 2 * RANK
OWN = SEQ // NP
WIN = NZ * NY // 2 * NC
TOK = OWN * LEN
PICK = OWN * LOSS
HALF = RANK // 2
FPZ = HALF // NZ
DEEP = FPZ * LANES
ROWS = NX * OWN
PER = 4
GP = 2
NG = NP // GP
SLOT = (0, 1, 7, 2, 6, 3, 5, 4)
PAIRS = NZ // 2
CHUNKS = ((2, 1), (1, 1), (3, 1), (0, 1), (2, 0), (1, 0), (3, 0), (0, 0))
BY_Y = 112
BY_X = PICK - BY_Y


def iota(shape, dim):
    return lax.broadcasted_iota(jnp.int32, shape, dim)


def split(v):
    hi = v.astype(BF16)
    return hi, (v - hi.astype(F32)).astype(BF16)


def mm(a, b, dims=((1,), (0,))):
    return lax.dot_general(a, b, (dims, ((), ())), preferred_element_type=F32)


def kernel(
    acts, grads, pos_hbm, in_hbm, out_hbm, window_hbm, out,
    pos, w_both, tokens, wbuf, hots, sbuf, y_part, x_part, x_sum, y_sum, fbuf, rowbuf, colbuf,
    lhs_hi, lhs_lo, rhs, turned_gram, pbuf, near, fin, window,
    beyond, in_sem, loc_sem, a_s, a_r, z_s, z_r, x_s, x_r, y_s, y_r, c_s, c_r, n_s, n_r, f_s, f_r,
):
    p, e = lax.axis_index("param"), lax.axis_index("example")
    yl, x = p // NX, p % NX
    z, yh, c = e // 4, (e // 2) % 2, e % 2
    y = yh * 2 + yl

    def dev(p_, e_):
        return {"param": p_, "example": e_}

    def p_at(dx, dyl):
        return ((yl + dyl) % 2) * NX + (x + dx) % NX

    def e_at(k):
        return ((z + k) % NZ) * 4 + yh * 2 + c

    def at_y(k):
        y_ = (y + k) % NY
        return dev((y_ % 2) * NX + x, z * 4 + (y_ // 2) * 2 + c)

    partner = dev(p, z * 4 + yh * 2 + (1 - c))

    def remote(src, dst, send, recv, to):
        return pltpu.make_async_remote_copy(
            src, dst, send, recv, device_id=to, device_id_type=MESH
        )

    def all_arrived(ref, sem):
        remote(ref, ref, sem, sem, partner).wait_recv()

    def all_sent(ref, sem):
        remote(ref, ref, sem, sem, partner).wait_send()

    order = [p_at(*d) for d in CHUNKS]

    def fetch_next(i):
        if i < NP:
            at = pl.ds(pl.multiple_of(order[i] * OWN, OWN), OWN)
            for k, src in enumerate((acts, grads)):
                pltpu.make_async_copy(src.at[at], tokens.at[i, k], in_sem.at[i % 3]).start()

    get_factors = [
        pltpu.make_async_copy(pos_hbm, pos, loc_sem.at[2]),
        pltpu.make_async_copy(in_hbm, w_both.at[pl.ds(0, RANK)], loc_sem.at[3]),
        pltpu.make_async_copy(out_hbm, w_both.at[pl.ds(RANK, RANK)], loc_sem.at[3]),
    ]
    for get in get_factors:
        get.start()
    fetch_next(0)
    get_window = pltpu.make_async_copy(window_hbm, window, loc_sem.at[1])
    barrier = pltpu.get_barrier_semaphore()
    others = [dev(p_at(k, 0), e) for k in (2, 1, 3)] + [dev(p, e_at(k)) for k in (2, 6, 1, 7)]
    others += [at_y(k) for k in (2, 1, 3)] + [partner]
    for d in others:
        pl.semaphore_signal(barrier, inc=1, device_id=d, device_id_type=MESH)

    fetch_next(1)
    fetch_next(2)
    get_window.start()
    pick_t = (iota((PICK, LOSS), 0) % LOSS == iota((PICK, LOSS), 1)).astype(F32).astype(BF16)
    lane = iota((PICK, TOK), 1)
    own_seq = iota((PICK, TOK), 0) // LOSS == lane // LEN
    token = jnp.where(own_seq, lane % LEN, -1).astype(F32)
    spread_at = iota((SEQ, TOK), 0) - iota((SEQ, TOK), 1) // LEN
    get_factors[0].wait()
    pos_t = mm(pick_t, pos[...].astype(F32).astype(BF16)).astype(BF16)
    for i in range(NP):
        spread = (spread_at == order[i] * OWN).astype(F32).astype(BF16)
        hots[i] = (mm(pos_t, spread) == token).astype(F32).astype(BF16)
    pltpu.make_async_copy(w_both, w_both, loc_sem.at[3]).wait()
    both = w_both[...].astype(F32).T
    low = iota(both.shape, 1) < RANK
    wbuf[0] = jnp.where(low, both, 0.0).astype(BF16)
    wbuf[1] = jnp.where(low, 0.0, both).astype(BF16)

    def to_yl(i):
        dx = CHUNKS[i][0]
        return remote(
            sbuf.at[i, pl.ds(0, BY_Y)], y_part.at[dx], a_s.at[0], a_r.at[dx], dev(p_at(0, 1), e)
        )

    def to_own_x(i):
        dx, dyl = CHUNKS[i]
        return remote(
            sbuf.at[i, pl.ds(BY_Y, BY_X)], x_part.at[dyl, dx], a_s.at[0], a_r.at[4 + dyl],
            dev(p_at(dx, 0), e),
        )

    def sum_to_x(i):
        dx = CHUNKS[i][0]
        return remote(
            sbuf.at[i, pl.ds(0, BY_Y)], x_sum.at[dx], a_s.at[0], a_r.at[6], dev(p_at(dx, 0), e)
        )

    def sum_to_yl():
        return remote(
            sbuf.at[3, pl.ds(BY_Y, BY_X)], y_sum, a_s.at[0], a_r.at[7], dev(p_at(0, 1), e)
        )

    def send_part(i):
        dx, dyl = CHUNKS[i]
        if dyl:
            to_yl(i).start()
        if dx:
            to_own_x(i).start()

    def project(i):
        pltpu.make_async_copy(tokens.at[i], tokens.at[i], in_sem.at[i % 3]).wait()
        fetch_next(i + 3)
        return mm(tokens[i, 0].reshape(TOK, -1), wbuf[0]) + mm(tokens[i, 1].reshape(TOK, -1), wbuf[1])

    def pick(i, ab):
        hi, lo = split(ab)
        return mm(hots[i], hi) + mm(hots[i], lo)

    ab = None
    for i in range(NP):
        ab, before = project(i), ab
        if i > 1:
            sbuf[i - 1] = pick(i - 1, before)
            send_part(i - 1)
        if i == 0:
            sbuf[0] = pick(0, ab)
            pl.semaphore_wait(barrier, len(others))
            send_part(0)
            for k in (2, 6):
                pl.semaphore_signal(beyond, inc=1, device_id=dev(p, e_at(k)), device_id_type=MESH)
    own = pick(NP - 1, ab)
    own_y, own_x = own[:BY_Y], own[BY_Y:]
    for i in (4, 5):
        to_yl(i - 4).wait_recv()
        sbuf[i, :BY_Y] = sbuf[i, :BY_Y] + y_part[CHUNKS[i][0]]
        sum_to_x(i).start()
    all_arrived(x_part.at[1, pl.ds(1, 3)], a_r.at[5])
    sbuf[3, BY_Y:] = sbuf[3, BY_Y:] + (x_part[1, 2] + (x_part[1, 1] + x_part[1, 3]))
    sum_to_yl().start()
    to_yl(2).wait_recv()
    sbuf[6, :BY_Y] = sbuf[6, :BY_Y] + y_part[3]
    sum_to_x(6).start()
    to_yl(3).wait_recv()
    own_y = own_y + y_part[0]
    all_arrived(x_part.at[0, pl.ds(1, 3)], a_r.at[4])
    own_x = own_x + (x_part[0, 2] + (x_part[0, 1] + x_part[0, 3]))
    all_arrived(x_sum.at[pl.ds(1, 3)], a_r.at[6])
    own_y = own_y + (x_sum[2] + (x_sum[1] + x_sum[3]))
    sum_to_yl().wait_recv()
    total = jnp.concatenate([own_y, own_x + y_sum[...]], axis=0)

    b_t = total.T[RANK:]
    in_seq = iota((OWN, PICK), 1) // LOSS == iota((OWN, PICK), 0)
    a_low = jnp.where(iota((PICK, LANES), 1) < RANK, total, 0.0)
    feats = jnp.zeros((HALF * OWN, LANES), F32)
    for h in range(2):
        b_h = b_t[h * HALF : (h + 1) * HALF]
        b_hi, b_lo = split(jnp.where(in_seq[None], b_h[:, None, :], 0.0).reshape(HALF * OWN, PICK))
        a_hi, a_lo = split(a_low if h == 0 else pltpu.roll(a_low, RANK, 1))
        feats = feats + (mm(b_hi, a_hi) + (mm(b_hi, a_lo) + mm(b_lo, a_hi)))
    fbuf[...] = feats.reshape(HALF, OWN, LANES)

    def tiles(j):
        z_ = (z + SLOT[j]) % NZ
        return remote(
            fbuf.at[pl.ds(z_ * FPZ, FPZ)], rowbuf.at[x, z], z_s.at[0], z_r.at[z // 2], dev(p, e_at(SLOT[j]))
        )

    pl.semaphore_wait(beyond, 2)
    for j in (7, 6, 5, 4, 3, 2, 1):
        tiles(j).start()
    pltpu.make_async_copy(fbuf.at[pl.ds(z * FPZ, FPZ)], rowbuf.at[x, z], z_r.at[z // 2]).start()

    def of_pair(h):
        return pl.ds(pl.multiple_of(pairs[h] * 2, 2), 2)

    step = jnp.where(z % 2 == 0, 3, 1)
    pairs = (z // 2, (z // 2 + step) % 4, (z // 2 + 4 - step) % 4, (z // 2 + 2) % 4)

    def to_x(k, h):
        at = of_pair(h)
        return remote(
            rowbuf.at[x, at], rowbuf.at[x, at], x_s.at[0], x_r.at[0], dev(p_at(k, 0), e)
        )

    def to_y(k, h):
        at = of_pair(h)
        return remote(rowbuf.at[x, at], colbuf.at[y, c, at], y_s.at[0], y_r.at[k, h], at_y(k))

    def from_y(k, h):
        at, y_ = of_pair(h), (y + NY - k) % NY
        return remote(rowbuf.at[x, at], colbuf.at[y_, c, at], y_s.at[0], y_r.at[k, h], at_y(k))

    def to_core(k, h):
        at, y_ = of_pair(h), (y + NY - k) % NY
        src = rowbuf.at[x, at] if k == 0 else colbuf.at[y_, c, at]
        return remote(src, colbuf.at[y_, c, at], c_s.at[0], c_r.at[(y_ // 2 + yh) % 2], partner)

    for h in range(PAIRS):
        all_arrived(rowbuf.at[x, of_pair(h)], z_r.at[pairs[h]])
        for k in (1, 3, 2):
            to_y(k, h).start()
            to_x(k, h).start()
        to_core(0, h).start()
    own_cols = pltpu.make_async_copy(rowbuf.at[x], colbuf.at[y, c], loc_sem.at[0])
    own_cols.start()
    for h in range(PAIRS):
        for k in (1, 3, 2):
            from_y(k, h).wait_recv()
            to_core(k, h).start()
    all_arrived(rowbuf.at[pl.ds(0, 3)], x_r.at[0])
    for i in range(FPZ):
        rows = jnp.concatenate([rowbuf[:, (z + SLOT[j]) % NZ, i].reshape(ROWS, LANES) for j in range(NZ)], axis=0)
        hi, lo = split(rows.T)
        lhs_hi[pl.ds(i * LANES, LANES)] = hi
        lhs_lo[pl.ds(i * LANES, LANES)] = lo
    def products(c_, yhs):
        n = len(yhs) * NZ * 2 * OWN

        def columns(z_, _):
            for k, yh_ in enumerate(yhs):
                at = pl.multiple_of((k * NZ + z_) * 2 * OWN, 2 * OWN)
                for i in range(FPZ):
                    v = jnp.concatenate([colbuf[yh_ * 2, c_, z_, i], colbuf[yh_ * 2 + 1, c_, z_, i]], axis=0)
                    hi, lo = split(v)
                    rhs[pl.ds(at, 2 * OWN), i * LANES : (i + 1) * LANES] = hi
                    rhs[pl.ds(n + at, 2 * OWN), i * LANES : (i + 1) * LANES] = lo
            return 0

        lax.fori_loop(0, NZ, columns, 0)
        both = mm(rhs[: 2 * n], lhs_hi[...])
        part = both[:n] + (both[n:] + mm(rhs[:n], lhs_lo[...]))
        for k, yh_ in enumerate(yhs):
            rows = part[k * NZ * 2 * OWN : (k + 1) * NZ * 2 * OWN]
            turned_gram[c_, yh_] = rows.reshape(NZ, 2 * OWN, NZ * ROWS)

    own_cols.wait()
    products(c, (0, 1))
    all_arrived(colbuf.at[pl.ds(0, 2), 0], c_r.at[0])
    products(1 - c, (yh,))
    all_arrived(colbuf.at[pl.ds(0, 2), 0], c_r.at[1])
    products(1 - c, (1 - yh,))
    get_window.wait()

    bit = iota((2 * OWN, LANES), 1) // 32

    def swap(a, b, n, shift):
        low = bit // n % 2 == 0
        return jnp.where(low, a, pltpu.roll(b, shift, 1)), jnp.where(low, pltpu.roll(a, LANES - shift, 1), b)

    def pack(g):
        for u in range(GP):
            es = [window[(g * GP + u) * PER + w] for w in range(PER)]
            for t in range(2):
                one = [
                    turned_gram[e_ % 2, (e_ // 2) % 2, e_ // 4, :, t * LANES : (t + 1) * LANES] for e_ in es
                ]
                even01, odd01 = swap(one[0], one[1], 1, 32)
                even23, odd23 = swap(one[2], one[3], 1, 32)
                by0, by2 = swap(even01, even23, 2, 64)
                by1, by3 = swap(odd01, odd23, 2, 64)
                for j, by in enumerate((by0, by1, by2, by3)):
                    pbuf[t * 4 + j, g * GP + u] = by

    def group(n):
        return (p // GP + n) % NG

    def to_near(i, n):
        at = pl.ds(group(n) * GP, GP)
        if i < 2:
            return remote(
                pbuf.at[5 + i, at], near.at[i, at], n_s.at[0], n_r.at[n], dev(p, e_at((1, 7)[i]))
            )
        k = jnp.where(group(n) < NG // 2, 6, 2)
        return remote(pbuf.at[7, at], near.at[2, at], n_s.at[0], n_r.at[n], dev(p, e_at(k)))

    def block_to(j, n, u):
        back = SLOT.index(-SLOT[j] % NZ)
        p_ = group(n) * GP + u
        at = back * NP + (p_ + NP - p) % NP
        return remote(pbuf.at[j, p_], fin.at[at], f_s.at[0], f_r.at[0], dev(p_, e_at(SLOT[j])))

    def send_blocks(n, js):
        for u in range(GP):
            for j in js:
                if j:
                    block_to(j, n, u).start()
                else:

                    @pl.when(group(n) * GP + u != p)
                    def _():
                        block_to(j, n, u).start()

    def far_rows(n, _):
        pack(group(n))
        for i in (2, 0, 1):
            to_near(i, n).start()
        return 0

    def near_rows(n, _):
        send_blocks(n, (1, 2, 0))
        return 0

    def merge(n, _):
        at = pl.ds(group(n) * GP, GP)
        all_arrived(near.at[:, at], n_r.at[n])
        below = group(n) < NG // 2
        pbuf[3, at] = pbuf[3, at] + (near[0, at] + jnp.where(below, 0.0, near[2, at]))
        pbuf[4, at] = pbuf[4, at] + (near[1, at] + jnp.where(below, near[2, at], 0.0))
        send_blocks(n, (3, 4))
        return 0

    lax.fori_loop(0, NG, far_rows, 0)
    lax.fori_loop(0, NG, near_rows, 0)
    fin[0] = pbuf[0, p]
    lax.fori_loop(0, NG, merge, 0)
    all_arrived(fin.at[pl.ds(1, 5 * NP - 1)], f_r.at[0])

    def gram_from(p_):
        i = (p + NP - p_) % NP
        return (fin[i] + (fin[NP + i] + fin[2 * NP + i])) + (fin[3 * NP + i] + fin[4 * NP + i])

    gram = [gram_from(p_) for p_ in range(NP)]
    turned = jnp.concatenate(
        [
            gram[yl_ * NX + i][k * OWN : (k + 1) * OWN]
            for yl_ in range(2)
            for k in range(2)
            for i in range(NX)
        ],
        axis=0,
    ).T
    low = iota((ROWS, LANES), 1) < SEQ
    for t in range(2):
        a, b = turned[t * 64 : t * 64 + 32], turned[t * 64 + 32 : t * 64 + 64]
        out[:ROWS, t * LANES : (t + 1) * LANES] = jnp.where(low, a, pltpu.roll(b, SEQ, 1))
        out[ROWS:, t * LANES : (t + 1) * LANES] = jnp.where(low, pltpu.roll(a, SEQ, 1), b)
    all_sent(sbuf, a_s.at[0])
    all_sent(rowbuf.at[0, pl.ds(0, NZ - 1)], z_s.at[0])
    all_sent(rowbuf.at[pl.ds(0, 3)], x_s.at[0])
    all_sent(rowbuf.at[pl.ds(0, 3)], y_s.at[0])
    all_sent(rowbuf, c_s.at[0])
    all_sent(near, n_s.at[0])
    all_sent(fin.at[pl.ds(1, 5 * NP - 1)], f_s.at[0])


def per_device(acts, grads, positions, proj_in, proj_out, window):
    depth = acts.shape[2]
    vmem, dma = pltpu.VMEM, pltpu.SemaphoreType.DMA
    in_vmem, in_hbm = pl.BlockSpec(memory_space=pltpu.VMEM), pl.BlockSpec(memory_space=pltpu.HBM)
    tile = (NZ, FPZ, OWN, LANES)
    scratch = [
        vmem((LOSS, SEQ), jnp.int32),
        vmem((LANES, depth), BF16),
        vmem((NP, 2, OWN, LEN, depth), BF16),
        vmem((2, depth, LANES), BF16),
        vmem((NP, PICK, TOK), BF16),
        vmem((NP - 1, PICK, LANES), F32),
        vmem((NX, BY_Y, LANES), F32),
        vmem((2, NX, BY_X, LANES), F32),
        vmem((NX, BY_Y, LANES), F32),
        vmem((BY_X, LANES), F32),
        vmem((HALF, OWN, LANES), F32),
        vmem((NX, *tile), F32),
        vmem((NY, NC, *tile), F32),
        vmem((DEEP, NZ * ROWS), BF16),
        vmem((DEEP, NZ * ROWS), BF16),
        vmem((4 * NZ * 2 * OWN, DEEP), BF16),
        vmem((NC, 2, NZ, 2 * OWN, NZ * ROWS), F32),
        vmem((NZ, NP, 2 * OWN, LANES), F32),
        vmem((3, NP, 2 * OWN, LANES), F32),
        vmem((5 * NP, 2 * OWN, LANES), F32),
        pltpu.SMEM((WIN,), jnp.int32),
        pltpu.SemaphoreType.REGULAR, dma((3,)), dma((4,)),
        dma((1,)), dma((8,)), dma((1,)), dma((4,)), dma((1,)), dma((1,)),
        dma((1,)), dma((NY, PAIRS)), dma((1,)), dma((2,)), dma((1,)), dma((NG,)),
        dma((1,)), dma((1,)),
    ]
    operands = (acts, grads, positions.T, proj_in.T, proj_out.T, window)
    return pl.pallas_call(
        kernel,
        out_shape=jax.ShapeDtypeStruct((SEQ, 4 * SEQ), F32),
        in_specs=[in_hbm] * 6,
        out_specs=in_vmem,
        scratch_shapes=scratch,
        name="similarity",
        cost_estimate=pl.CostEstimate(flops=1_000_000_000, bytes_accessed=9_000_000, transcendentals=0),
        compiler_params=pltpu.CompilerParams(
            collective_id=0, has_side_effects=True, vmem_limit_bytes=40 << 20
        ),
    )(*(pltpu.with_memory_space_constraint(v, pltpu.HBM) for v in operands))


def solution(mesh):
    in_specs = (
        P("example", None, "param"),
        P("example", None, "param"),
        P("example", None),
        P("param", None),
        P("param", None),
        P(),
    )
    return jax.shard_map(
        per_device, mesh=mesh, in_specs=in_specs, out_specs=P("example", "param"), check_vma=False
    )
```

```python
import jax
import jax.numpy as jnp
from jax import lax
from jax.experimental import pallas as pl
from jax.experimental.pallas import tpu as pltpu
from jax.sharding import PartitionSpec as P

F32, BF16 = jnp.float32, jnp.bfloat16
MESH = pl.DeviceIdType.MESH
NT = ((1,), (1,))

NP, NX, NY, NZ, NC = 8, 4, 4, 8, 2
SEQ, LEN, LOSS, RANK = 64, 32, 24, 64
LANES = 2 * RANK
OWN = SEQ // NP
WIN = NZ * NY // 2 * NC
TOK = OWN * LEN
PICK = OWN * LOSS
HALF = RANK // 2
FPZ = HALF // NZ
DEEP = FPZ * LANES
ROWS = NX * OWN
PER = 4
WIDE = 4 * OWN
GP = 2
NG = NP // GP
SLOT = (0, 1, 7, 2, 6, 3, 5, 4)
PAIRS = NZ // 2
CHUNKS = ((2, 1), (1, 1), (3, 1), (0, 1), (2, 0), (1, 0), (3, 0), (0, 0))
BY_Y = 112
BY_X = PICK - BY_Y


def iota(shape, dim):
    return lax.broadcasted_iota(jnp.int32, shape, dim)


def split(v):
    hi = v.astype(BF16)
    return hi, (v - hi.astype(F32)).astype(BF16)


def mm(a, b, dims=((1,), (0,))):
    return lax.dot_general(a, b, (dims, ((), ())), preferred_element_type=F32)


def kernel(
    acts, grads, pos_hbm, in_hbm, out_hbm, window_hbm, out,
    pos, w_both, tokens, wbuf, hots, sbuf, y_part, x_part, x_sum, y_sum, fbuf, rowbuf, colbuf,
    lhs_hi, lhs_lo, rhs, turned_gram, pbuf, near, fin, window,
    beyond, in_sem, loc_sem, a_s, a_r, z_s, z_r, x_s, x_r, y_s, y_r, c_s, c_r, n_s, n_r, f_s, f_r,
):
    p, e = lax.axis_index("param"), lax.axis_index("example")
    yl, x = p // NX, p % NX
    z, yh, c = e // 4, (e // 2) % 2, e % 2
    y = yh * 2 + yl

    def dev(p_, e_):
        return {"param": p_, "example": e_}

    def p_at(dx, dyl):
        return ((yl + dyl) % 2) * NX + (x + dx) % NX

    def e_at(k):
        return ((z + k) % NZ) * 4 + yh * 2 + c

    def at_y(k):
        y_ = (y + k) % NY
        return dev((y_ % 2) * NX + x, z * 4 + (y_ // 2) * 2 + c)

    partner = dev(p, z * 4 + yh * 2 + (1 - c))

    def remote(src, dst, send, recv, to):
        return pltpu.make_async_remote_copy(
            src, dst, send, recv, device_id=to, device_id_type=MESH
        )

    def all_arrived(ref, sem):
        remote(ref, ref, sem, sem, partner).wait_recv()

    def all_sent(ref, sem):
        remote(ref, ref, sem, sem, partner).wait_send()

    order = [p_at(*d) for d in CHUNKS]

    def fetch_next(i):
        if i < NP:
            at = pl.ds(pl.multiple_of(order[i] * OWN, OWN), OWN)
            for k, src in enumerate((acts, grads)):
                pltpu.make_async_copy(src.at[at], tokens.at[i, k], in_sem.at[i % 3]).start()

    get_factors = [
        pltpu.make_async_copy(pos_hbm, pos, loc_sem.at[2]),
        pltpu.make_async_copy(in_hbm, w_both.at[pl.ds(0, RANK)], loc_sem.at[3]),
        pltpu.make_async_copy(out_hbm, w_both.at[pl.ds(RANK, RANK)], loc_sem.at[3]),
    ]
    for get in get_factors:
        get.start()
    fetch_next(0)
    get_window = pltpu.make_async_copy(window_hbm, window, loc_sem.at[1])
    barrier = pltpu.get_barrier_semaphore()
    others = [dev(p_at(k, 0), e) for k in (2, 1, 3)] + [dev(p, e_at(k)) for k in (2, 6, 1, 7)]
    others += [at_y(k) for k in (2, 1, 3)] + [partner]
    for d in others:
        pl.semaphore_signal(barrier, inc=1, device_id=d, device_id_type=MESH)

    fetch_next(1)
    fetch_next(2)
    get_window.start()
    pick_t = (iota((PICK, LOSS), 0) % LOSS == iota((PICK, LOSS), 1)).astype(F32).astype(BF16)
    lane = iota((PICK, TOK), 1)
    own_seq = iota((PICK, TOK), 0) // LOSS == lane // LEN
    token = jnp.where(own_seq, lane % LEN, -1).astype(F32)
    spread_at = iota((SEQ, TOK), 0) - iota((SEQ, TOK), 1) // LEN
    get_factors[0].wait()
    pos_t = mm(pick_t, pos[...].astype(F32).astype(BF16)).astype(BF16)

    def find(i):
        spread = (spread_at == order[i] * OWN).astype(F32).astype(BF16)
        hots[i] = (mm(pos_t, spread) == token).astype(F32).astype(BF16)
    find(0)
    pltpu.make_async_copy(w_both, w_both, loc_sem.at[3]).wait()
    both = w_both[...].astype(F32).T
    low = iota(both.shape, 1) < RANK
    wbuf[0] = jnp.where(low, both, 0.0).astype(BF16)
    wbuf[1] = jnp.where(low, 0.0, both).astype(BF16)

    def to_yl(i):
        dx = CHUNKS[i][0]
        return remote(
            sbuf.at[i, pl.ds(0, BY_Y)], y_part.at[dx], a_s.at[0], a_r.at[dx], dev(p_at(0, 1), e)
        )

    def to_own_x(i):
        dx, dyl = CHUNKS[i]
        return remote(
            sbuf.at[i, pl.ds(BY_Y, BY_X)], x_part.at[dyl, dx], a_s.at[0], a_r.at[4 + dyl],
            dev(p_at(dx, 0), e),
        )

    def sum_to_x(i):
        dx = CHUNKS[i][0]
        return remote(
            sbuf.at[i, pl.ds(0, BY_Y)], x_sum.at[dx], a_s.at[0], a_r.at[6], dev(p_at(dx, 0), e)
        )

    def sum_to_yl():
        return remote(
            sbuf.at[3, pl.ds(BY_Y, BY_X)], y_sum, a_s.at[0], a_r.at[7], dev(p_at(0, 1), e)
        )

    def send_part(i):
        dx, dyl = CHUNKS[i]
        if dyl:
            to_yl(i).start()
        if dx:
            to_own_x(i).start()

    def project(i):
        pltpu.make_async_copy(tokens.at[i], tokens.at[i], in_sem.at[i % 3]).wait()
        fetch_next(i + 3)
        return mm(tokens[i, 0].reshape(TOK, -1), wbuf[0]) + mm(tokens[i, 1].reshape(TOK, -1), wbuf[1])

    def pick(i, ab):
        hi, lo = split(ab)
        return mm(hots[i], hi) + mm(hots[i], lo)

    ab = None
    for i in range(NP):
        if i:
            find(i)
        ab, before = project(i), ab
        if i > 1:
            sbuf[i - 1] = pick(i - 1, before)
            send_part(i - 1)
        if i == 0:
            sbuf[0] = pick(0, ab)
            pl.semaphore_wait(barrier, len(others))
            send_part(0)
            for k in (2, 6):
                pl.semaphore_signal(beyond, inc=1, device_id=dev(p, e_at(k)), device_id_type=MESH)
    own = pick(NP - 1, ab)
    own_y, own_x = own[:BY_Y], own[BY_Y:]
    for i in (4, 5):
        to_yl(i - 4).wait_recv()
        sbuf[i, :BY_Y] = sbuf[i, :BY_Y] + y_part[CHUNKS[i][0]]
        sum_to_x(i).start()
    all_arrived(x_part.at[1, pl.ds(1, 3)], a_r.at[5])
    sbuf[3, BY_Y:] = sbuf[3, BY_Y:] + (x_part[1, 2] + (x_part[1, 1] + x_part[1, 3]))
    sum_to_yl().start()
    to_yl(2).wait_recv()
    sbuf[6, :BY_Y] = sbuf[6, :BY_Y] + y_part[3]
    sum_to_x(6).start()
    to_yl(3).wait_recv()
    own_y = own_y + y_part[0]
    all_arrived(x_part.at[0, pl.ds(1, 3)], a_r.at[4])
    own_x = own_x + (x_part[0, 2] + (x_part[0, 1] + x_part[0, 3]))
    all_arrived(x_sum.at[pl.ds(1, 3)], a_r.at[6])
    own_y = own_y + (x_sum[2] + (x_sum[1] + x_sum[3]))
    sum_to_yl().wait_recv()
    total = jnp.concatenate([own_y, own_x + y_sum[...]], axis=0)

    b_t = total.T[RANK:]
    in_seq = iota((OWN, PICK), 1) // LOSS == iota((OWN, PICK), 0)
    a_low = jnp.where(iota((PICK, LANES), 1) < RANK, total, 0.0)
    feats = jnp.zeros((HALF * OWN, LANES), F32)
    for h in range(2):
        b_h = b_t[h * HALF : (h + 1) * HALF]
        b_hi, b_lo = split(jnp.where(in_seq[None], b_h[:, None, :], 0.0).reshape(HALF * OWN, PICK))
        a_hi, a_lo = split(a_low if h == 0 else pltpu.roll(a_low, RANK, 1))
        feats = feats + (mm(b_hi, a_hi) + (mm(b_hi, a_lo) + mm(b_lo, a_hi)))
    fbuf[...] = feats.reshape(HALF, OWN, LANES)

    def tiles(j):
        z_ = (z + SLOT[j]) % NZ
        return remote(
            fbuf.at[pl.ds(z_ * FPZ, FPZ)], rowbuf.at[x, z], z_s.at[0], z_r.at[z // 2], dev(p, e_at(SLOT[j]))
        )

    pl.semaphore_wait(beyond, 2)
    for j in (7, 6, 5, 4, 3, 2, 1):
        tiles(j).start()
    pltpu.make_async_copy(fbuf.at[pl.ds(z * FPZ, FPZ)], rowbuf.at[x, z], z_r.at[z // 2]).start()

    def of_pair(h):
        return pl.ds(pl.multiple_of(pairs[h] * 2, 2), 2)

    step = jnp.where(z % 2 == 0, 3, 1)
    pairs = (z // 2, (z // 2 + step) % 4, (z // 2 + 4 - step) % 4, (z // 2 + 2) % 4)

    def to_x(k, h):
        at = of_pair(h)
        return remote(
            rowbuf.at[x, at], rowbuf.at[x, at], x_s.at[0], x_r.at[0], dev(p_at(k, 0), e)
        )

    def to_y(k, h):
        at = of_pair(h)
        return remote(rowbuf.at[x, at], colbuf.at[y, c, at], y_s.at[0], y_r.at[k, h], at_y(k))

    def from_y(k, h):
        at, y_ = of_pair(h), (y + NY - k) % NY
        return remote(rowbuf.at[x, at], colbuf.at[y_, c, at], y_s.at[0], y_r.at[k, h], at_y(k))

    def to_core(k, h):
        at, y_ = of_pair(h), (y + NY - k) % NY
        src = rowbuf.at[x, at] if k == 0 else colbuf.at[y_, c, at]
        return remote(src, colbuf.at[y_, c, at], c_s.at[0], c_r.at[h // 2], partner)

    for h in range(PAIRS):
        all_arrived(rowbuf.at[x, of_pair(h)], z_r.at[pairs[h]])
        for k in (1, 3, 2):
            to_y(k, h).start()
            to_x(k, h).start()
        to_core(0, h).start()
    own_cols = pltpu.make_async_copy(rowbuf.at[x], colbuf.at[y, c], loc_sem.at[0])
    own_cols.start()
    for h in range(PAIRS):
        for k in (1, 3, 2):
            from_y(k, h).wait_recv()
            to_core(k, h).start()
    def prepare(c_, zs):
        n = len(zs) * WIDE

        def columns(yh_, _):
            for k, z_ in enumerate(zs):
                at = pl.multiple_of(k * WIDE + yh_ * 2 * OWN, 2 * OWN)
                for i in range(FPZ):
                    v = jnp.concatenate([colbuf[yh_ * 2, c_, z_, i], colbuf[yh_ * 2 + 1, c_, z_, i]], axis=0)
                    hi, lo = split(v)
                    rhs[pl.ds(at, 2 * OWN), i * LANES : (i + 1) * LANES] = hi
                    rhs[pl.ds(n + at, 2 * OWN), i * LANES : (i + 1) * LANES] = lo
            return 0

        lax.fori_loop(0, 2, columns, 0)

    def products(c_, zs):
        n = len(zs) * WIDE
        both = mm(rhs[: 2 * n], lhs_hi[...])
        part = both[:n] + (both[n:] + mm(rhs[:n], lhs_lo[...]))
        for k, z_ in enumerate(zs):
            turned_gram[c_, z_] = part[k * WIDE : (k + 1) * WIDE].reshape(2, 2 * OWN, NZ * ROWS)

    own_cols.wait()
    prepare(c, range(NZ))
    all_arrived(rowbuf.at[pl.ds(0, 3)], x_r.at[0])
    for i in range(FPZ):
        rows = jnp.concatenate([rowbuf[:, (z + SLOT[j]) % NZ, i].reshape(ROWS, LANES) for j in range(NZ)], axis=0)
        hi, lo = split(rows.T)
        lhs_hi[pl.ds(i * LANES, LANES)] = hi
        lhs_lo[pl.ds(i * LANES, LANES)] = lo
    products(c, range(NZ))
    all_arrived(colbuf.at[pl.ds(0, 2), 0], c_r.at[0])
    part = [pairs[h] * 2 + u for h in range(2) for u in range(2)]
    prepare(1 - c, part)
    products(1 - c, part)
    all_arrived(colbuf.at[pl.ds(0, 2), 0], c_r.at[1])
    part = [pairs[h] * 2 + u for h in range(2, 4) for u in range(2)]
    prepare(1 - c, part)
    products(1 - c, part)
    get_window.wait()

    bit = iota((2 * OWN, LANES), 1) // 32

    def swap(a, b, n, shift):
        low = bit // n % 2 == 0
        return jnp.where(low, a, pltpu.roll(b, shift, 1)), jnp.where(low, pltpu.roll(a, LANES - shift, 1), b)

    def pack(g):
        for u in range(GP):
            es = [window[(g * GP + u) * PER + w] for w in range(PER)]
            for t in range(2):
                one = [
                    turned_gram[e_ % 2, e_ // 4, (e_ // 2) % 2, :, t * LANES : (t + 1) * LANES] for e_ in es
                ]
                even01, odd01 = swap(one[0], one[1], 1, 32)
                even23, odd23 = swap(one[2], one[3], 1, 32)
                by0, by2 = swap(even01, even23, 2, 64)
                by1, by3 = swap(odd01, odd23, 2, 64)
                for j, by in enumerate((by0, by1, by2, by3)):
                    pbuf[t * 4 + j, g * GP + u] = by

    def group(n):
        return (yl + 1 - n // 2) % 2 * 2 + (x // GP + 1 - n % 2) % 2

    def to_near(i, n):
        at = pl.ds(group(n) * GP, GP)
        if i < 2:
            return remote(
                pbuf.at[5 + i, at], near.at[i, at], n_s.at[0], n_r.at[n], dev(p, e_at((1, 7)[i]))
            )
        k = jnp.where(group(n) < NG // 2, 6, 2)
        return remote(pbuf.at[7, at], near.at[2, at], n_s.at[0], n_r.at[n], dev(p, e_at(k)))

    def block_to(j, n, u):
        back = SLOT.index(-SLOT[j] % NZ)
        p_ = group(n) * GP + u
        at = back * NP + (p_ + NP - p) % NP
        return remote(pbuf.at[j, p_], fin.at[at], f_s.at[0], f_r.at[0], dev(p_, e_at(SLOT[j])))

    def send_blocks(n, js):
        for u in range(GP):
            for j in js:
                if j:
                    block_to(j, n, u).start()
                else:

                    @pl.when(group(n) * GP + u != p)
                    def _():
                        block_to(j, n, u).start()

    def far_rows(n, _):
        pack(group(n))
        for i in (2, 0, 1):
            to_near(i, n).start()
        return 0

    def near_rows(n, _):
        send_blocks(n, (1, 2, 0))
        return 0

    def merge(n, _):
        at = pl.ds(group(n) * GP, GP)
        all_arrived(near.at[:, at], n_r.at[n])
        below = group(n) < NG // 2
        pbuf[3, at] = pbuf[3, at] + (near[0, at] + jnp.where(below, 0.0, near[2, at]))
        pbuf[4, at] = pbuf[4, at] + (near[1, at] + jnp.where(below, near[2, at], 0.0))
        send_blocks(n, (3, 4))
        return 0

    lax.fori_loop(0, NG, far_rows, 0)
    lax.fori_loop(0, NG, near_rows, 0)
    fin[0] = pbuf[0, p]
    lax.fori_loop(0, NG, merge, 0)
    all_arrived(fin.at[pl.ds(1, 5 * NP - 1)], f_r.at[0])

    def gram_from(p_):
        i = (p + NP - p_) % NP
        return (fin[i] + (fin[NP + i] + fin[2 * NP + i])) + (fin[3 * NP + i] + fin[4 * NP + i])

    gram = [gram_from(p_) for p_ in range(NP)]
    turned = jnp.concatenate(
        [
            gram[yl_ * NX + i][k * OWN : (k + 1) * OWN]
            for yl_ in range(2)
            for k in range(2)
            for i in range(NX)
        ],
        axis=0,
    ).T
    low = iota((ROWS, LANES), 1) < SEQ
    for t in range(2):
        a, b = turned[t * 64 : t * 64 + 32], turned[t * 64 + 32 : t * 64 + 64]
        out[:ROWS, t * LANES : (t + 1) * LANES] = jnp.where(low, a, pltpu.roll(b, SEQ, 1))
        out[ROWS:, t * LANES : (t + 1) * LANES] = jnp.where(low, pltpu.roll(a, SEQ, 1), b)
    all_sent(sbuf, a_s.at[0])
    all_sent(rowbuf.at[0, pl.ds(0, NZ - 1)], z_s.at[0])
    all_sent(rowbuf.at[pl.ds(0, 3)], x_s.at[0])
    all_sent(rowbuf.at[pl.ds(0, 3)], y_s.at[0])
    all_sent(rowbuf, c_s.at[0])
    all_sent(near, n_s.at[0])
    all_sent(fin.at[pl.ds(1, 5 * NP - 1)], f_s.at[0])


def per_device(acts, grads, positions, proj_in, proj_out, window):
    depth = acts.shape[2]
    vmem, dma = pltpu.VMEM, pltpu.SemaphoreType.DMA
    in_vmem, in_hbm = pl.BlockSpec(memory_space=pltpu.VMEM), pl.BlockSpec(memory_space=pltpu.HBM)
    tile = (NZ, FPZ, OWN, LANES)
    scratch = [
        vmem((LOSS, SEQ), jnp.int32),
        vmem((LANES, depth), BF16),
        vmem((NP, 2, OWN, LEN, depth), BF16),
        vmem((2, depth, LANES), BF16),
        vmem((NP, PICK, TOK), BF16),
        vmem((NP - 1, PICK, LANES), F32),
        vmem((NX, BY_Y, LANES), F32),
        vmem((2, NX, BY_X, LANES), F32),
        vmem((NX, BY_Y, LANES), F32),
        vmem((BY_X, LANES), F32),
        vmem((HALF, OWN, LANES), F32),
        vmem((NX, *tile), F32),
        vmem((NY, NC, *tile), F32),
        vmem((DEEP, NZ * ROWS), BF16),
        vmem((DEEP, NZ * ROWS), BF16),
        vmem((4 * NZ * 2 * OWN, DEEP), BF16),
        vmem((NC, NZ, 2, 2 * OWN, NZ * ROWS), F32),
        vmem((NZ, NP, 2 * OWN, LANES), F32),
        vmem((3, NP, 2 * OWN, LANES), F32),
        vmem((5 * NP, 2 * OWN, LANES), F32),
        pltpu.SMEM((WIN,), jnp.int32),
        pltpu.SemaphoreType.REGULAR, dma((3,)), dma((4,)),
        dma((1,)), dma((8,)), dma((1,)), dma((4,)), dma((1,)), dma((1,)),
        dma((1,)), dma((NY, PAIRS)), dma((1,)), dma((2,)), dma((1,)), dma((NG,)),
        dma((1,)), dma((1,)),
    ]
    operands = (acts, grads, positions.T, proj_in.T, proj_out.T, window)
    return pl.pallas_call(
        kernel,
        out_shape=jax.ShapeDtypeStruct((SEQ, 4 * SEQ), F32),
        in_specs=[in_hbm] * 6,
        out_specs=in_vmem,
        scratch_shapes=scratch,
        name="similarity",
        cost_estimate=pl.CostEstimate(flops=1_000_000_000, bytes_accessed=9_000_000, transcendentals=0),
        compiler_params=pltpu.CompilerParams(
            collective_id=0, has_side_effects=True, vmem_limit_bytes=40 << 20
        ),
    )(*(pltpu.with_memory_space_constraint(v, pltpu.HBM) for v in operands))


def solution(mesh):
    in_specs = (
        P("example", None, "param"),
        P("example", None, "param"),
        P("example", None),
        P("param", None),
        P("param", None),
        P(),
    )
    return jax.shard_map(
        per_device, mesh=mesh, in_specs=in_specs, out_specs=P("example", "param"), check_vma=False
    )
```

```python
import jax
import jax.numpy as jnp
from jax import lax
from jax.experimental import pallas as pl
from jax.experimental.pallas import tpu as pltpu
from jax.sharding import PartitionSpec as P

F32, BF16 = jnp.float32, jnp.bfloat16
MESH = pl.DeviceIdType.MESH
NT = ((1,), (1,))

NP, NX, NY, NZ, NC = 8, 4, 4, 8, 2
SEQ, LEN, LOSS, RANK = 64, 32, 24, 64
LANES = 2 * RANK
OWN = SEQ // NP
WIN = NZ * NY // 2 * NC
TOK = OWN * LEN
PICK = OWN * LOSS
HALF = RANK // 2
FPZ = HALF // NZ
DEEP = FPZ * LANES
ROWS = NX * OWN
PER = 4
WIDE = 4 * OWN
GP = 2
NG = NP // GP
SLOT = (0, 1, 7, 2, 6, 3, 5, 4)
PAIRS = NZ // 2
CHUNKS = ((2, 1), (2, 0), (1, 1), (3, 1), (1, 0), (3, 0), (0, 1), (0, 0))
SAME, OTHER = ([CHUNKS.index((dx, dyl)) for dx in range(NX)] for dyl in range(2))
BY_Y = 112
BY_X = PICK - BY_Y


def iota(shape, dim):
    return lax.broadcasted_iota(jnp.int32, shape, dim)


def split(v):
    hi = v.astype(BF16)
    return hi, (v - hi.astype(F32)).astype(BF16)


def mm(a, b, dims=((1,), (0,))):
    return lax.dot_general(a, b, (dims, ((), ())), preferred_element_type=F32)


def kernel(
    acts, grads, pos_hbm, in_hbm, out_hbm, window_hbm, out,
    pos, w_both, tokens, wbuf, hots, sbuf, y_part, x_part, x_sum, y_sum, fbuf, rowbuf, colbuf,
    lhs_hi, lhs_lo, rhs, turned_gram, pbuf, near, fin, window,
    beyond, in_sem, loc_sem, a_s, a_r, z_s, z_r, x_s, x_r, y_s, y_r, c_s, c_r, n_s, n_r, f_s, f_r,
):
    p, e = lax.axis_index("param"), lax.axis_index("example")
    yl, x = p // NX, p % NX
    z, yh, c = e // 4, (e // 2) % 2, e % 2
    y = yh * 2 + yl

    def dev(p_, e_):
        return {"param": p_, "example": e_}

    def p_at(dx, dyl):
        return ((yl + dyl) % 2) * NX + (x + dx) % NX

    def e_at(k):
        return ((z + k) % NZ) * 4 + yh * 2 + c

    def at_y(k):
        y_ = (y + k) % NY
        return dev((y_ % 2) * NX + x, z * 4 + (y_ // 2) * 2 + c)

    partner = dev(p, z * 4 + yh * 2 + (1 - c))

    def remote(src, dst, send, recv, to):
        return pltpu.make_async_remote_copy(
            src, dst, send, recv, device_id=to, device_id_type=MESH
        )

    def all_arrived(ref, sem):
        remote(ref, ref, sem, sem, partner).wait_recv()

    def all_sent(ref, sem):
        remote(ref, ref, sem, sem, partner).wait_send()

    order = [p_at(*d) for d in CHUNKS]

    def fetch_next(i):
        if i < NP:
            at = pl.ds(pl.multiple_of(order[i] * OWN, OWN), OWN)
            for k, src in enumerate((acts, grads)):
                pltpu.make_async_copy(src.at[at], tokens.at[i, k], in_sem.at[i % 3]).start()

    get_factors = [
        pltpu.make_async_copy(pos_hbm, pos, loc_sem.at[2]),
        pltpu.make_async_copy(in_hbm, w_both.at[pl.ds(0, RANK)], loc_sem.at[3]),
        pltpu.make_async_copy(out_hbm, w_both.at[pl.ds(RANK, RANK)], loc_sem.at[3]),
    ]
    for get in get_factors:
        get.start()
    fetch_next(0)
    get_window = pltpu.make_async_copy(window_hbm, window, loc_sem.at[1])
    barrier = pltpu.get_barrier_semaphore()
    others = [dev(p_at(k, 0), e) for k in (2, 1, 3)] + [dev(p, e_at(k)) for k in (2, 6, 1, 7)]
    others += [at_y(k) for k in (2, 1, 3)] + [partner]
    for d in others:
        pl.semaphore_signal(barrier, inc=1, device_id=d, device_id_type=MESH)

    fetch_next(1)
    fetch_next(2)
    get_window.start()
    pick_t = (iota((PICK, LOSS), 0) % LOSS == iota((PICK, LOSS), 1)).astype(F32).astype(BF16)
    lane = iota((PICK, TOK), 1)
    own_seq = iota((PICK, TOK), 0) // LOSS == lane // LEN
    token = jnp.where(own_seq, lane % LEN, -1).astype(F32)
    spread_at = iota((SEQ, TOK), 0) - iota((SEQ, TOK), 1) // LEN
    get_factors[0].wait()
    pos_t = mm(pick_t, pos[...].astype(F32).astype(BF16)).astype(BF16)

    def find(i):
        spread = (spread_at == order[i] * OWN).astype(F32).astype(BF16)
        hots[i] = (mm(pos_t, spread) == token).astype(F32).astype(BF16)
    find(0)
    pltpu.make_async_copy(w_both, w_both, loc_sem.at[3]).wait()
    both = w_both[...].astype(F32).T
    low = iota(both.shape, 1) < RANK
    wbuf[0] = jnp.where(low, both, 0.0).astype(BF16)
    wbuf[1] = jnp.where(low, 0.0, both).astype(BF16)

    def to_yl(i):
        dx = CHUNKS[i][0]
        return remote(
            sbuf.at[i, pl.ds(0, BY_Y)], y_part.at[dx], a_s.at[0], a_r.at[dx], dev(p_at(0, 1), e)
        )

    def to_own_x(i):
        dx, dyl = CHUNKS[i]
        return remote(
            sbuf.at[i, pl.ds(BY_Y, BY_X)], x_part.at[dyl, dx], a_s.at[0], a_r.at[4 + dyl],
            dev(p_at(dx, 0), e),
        )

    def sum_to_x(i):
        dx = CHUNKS[i][0]
        return remote(
            sbuf.at[i, pl.ds(0, BY_Y)], x_sum.at[dx], a_s.at[0], a_r.at[6], dev(p_at(dx, 0), e)
        )

    def sum_to_yl():
        return remote(
            sbuf.at[OTHER[0], pl.ds(BY_Y, BY_X)], y_sum, a_s.at[0], a_r.at[7], dev(p_at(0, 1), e)
        )

    def send_part(i):
        dx, dyl = CHUNKS[i]
        if dyl:
            to_yl(i).start()
        if dx:
            to_own_x(i).start()

    def project(i):
        pltpu.make_async_copy(tokens.at[i], tokens.at[i], in_sem.at[i % 3]).wait()
        fetch_next(i + 3)
        return mm(tokens[i, 0].reshape(TOK, -1), wbuf[0]) + mm(tokens[i, 1].reshape(TOK, -1), wbuf[1])

    def pick(i, ab):
        hi, lo = split(ab)
        return mm(hots[i], hi) + mm(hots[i], lo)

    ab = None
    for i in range(NP):
        if i:
            find(i)
        ab, before = project(i), ab
        if i > 1:
            sbuf[i - 1] = pick(i - 1, before)
            send_part(i - 1)
        if i == 0:
            sbuf[0] = pick(0, ab)
            pl.semaphore_wait(barrier, len(others))
            send_part(0)
            for k in (2, 6):
                pl.semaphore_signal(beyond, inc=1, device_id=dev(p, e_at(k)), device_id_type=MESH)
    own = pick(NP - 1, ab)
    own_y, own_x = own[:BY_Y], own[BY_Y:]
    for dx in (2, 1):
        to_yl(OTHER[dx]).wait_recv()
        i = SAME[dx]
        sbuf[i, :BY_Y] = sbuf[i, :BY_Y] + y_part[dx]
        sum_to_x(i).start()
    all_arrived(x_part.at[1, pl.ds(1, 3)], a_r.at[5])
    i = OTHER[0]
    sbuf[i, BY_Y:] = sbuf[i, BY_Y:] + (x_part[1, 2] + (x_part[1, 1] + x_part[1, 3]))
    sum_to_yl().start()
    to_yl(OTHER[3]).wait_recv()
    i = SAME[3]
    sbuf[i, :BY_Y] = sbuf[i, :BY_Y] + y_part[3]
    sum_to_x(i).start()
    to_yl(OTHER[0]).wait_recv()
    own_y = own_y + y_part[0]
    all_arrived(x_part.at[0, pl.ds(1, 3)], a_r.at[4])
    own_x = own_x + (x_part[0, 2] + (x_part[0, 1] + x_part[0, 3]))
    all_arrived(x_sum.at[pl.ds(1, 3)], a_r.at[6])
    own_y = own_y + (x_sum[2] + (x_sum[1] + x_sum[3]))
    sum_to_yl().wait_recv()
    total = jnp.concatenate([own_y, own_x + y_sum[...]], axis=0)

    b_t = total.T[RANK:]
    in_seq = iota((OWN, PICK), 1) // LOSS == iota((OWN, PICK), 0)
    a_low = jnp.where(iota((PICK, LANES), 1) < RANK, total, 0.0)
    feats = jnp.zeros((HALF * OWN, LANES), F32)
    for h in range(2):
        b_h = b_t[h * HALF : (h + 1) * HALF]
        b_hi, b_lo = split(jnp.where(in_seq[None], b_h[:, None, :], 0.0).reshape(HALF * OWN, PICK))
        a_hi, a_lo = split(a_low if h == 0 else pltpu.roll(a_low, RANK, 1))
        feats = feats + (mm(b_hi, a_hi) + (mm(b_hi, a_lo) + mm(b_lo, a_hi)))
    fbuf[...] = feats.reshape(HALF, OWN, LANES)

    def tiles(j):
        z_ = (z + SLOT[j]) % NZ
        return remote(
            fbuf.at[pl.ds(z_ * FPZ, FPZ)], rowbuf.at[x, z], z_s.at[0], z_r.at[z // 2], dev(p, e_at(SLOT[j]))
        )

    pl.semaphore_wait(beyond, 2)
    for j in (7, 6, 5, 4, 3, 2, 1):
        tiles(j).start()
    pltpu.make_async_copy(fbuf.at[pl.ds(z * FPZ, FPZ)], rowbuf.at[x, z], z_r.at[z // 2]).start()

    def of_pair(h):
        return pl.ds(pl.multiple_of(pairs[h] * 2, 2), 2)

    step = jnp.where(z % 2 == 0, 3, 1)
    pairs = (z // 2, (z // 2 + step) % 4, (z // 2 + 4 - step) % 4, (z // 2 + 2) % 4)

    def to_x(k, h):
        at = of_pair(h)
        return remote(
            rowbuf.at[x, at], rowbuf.at[x, at], x_s.at[0], x_r.at[0], dev(p_at(k, 0), e)
        )

    def to_y(k, h):
        at = of_pair(h)
        return remote(rowbuf.at[x, at], colbuf.at[y, c, at], y_s.at[0], y_r.at[k, h], at_y(k))

    def from_y(k, h):
        at, y_ = of_pair(h), (y + NY - k) % NY
        return remote(rowbuf.at[x, at], colbuf.at[y_, c, at], y_s.at[0], y_r.at[k, h], at_y(k))

    def to_core(k, h):
        at, y_ = of_pair(h), (y + NY - k) % NY
        src = rowbuf.at[x, at] if k == 0 else colbuf.at[y_, c, at]
        return remote(src, colbuf.at[y_, c, at], c_s.at[0], c_r.at[h // 2], partner)

    for h in range(PAIRS):
        all_arrived(rowbuf.at[x, of_pair(h)], z_r.at[pairs[h]])
        for k in (1, 3, 2):
            to_y(k, h).start()
            to_x(k, h).start()
        to_core(0, h).start()
    own_cols = pltpu.make_async_copy(rowbuf.at[x], colbuf.at[y, c], loc_sem.at[0])
    own_cols.start()
    for h in range(PAIRS):
        for k in (1, 3, 2):
            from_y(k, h).wait_recv()
            to_core(k, h).start()
    def prepare(c_, zs):
        n = len(zs) * WIDE

        def columns(yh_, _):
            for k, z_ in enumerate(zs):
                at = pl.multiple_of(k * WIDE + yh_ * 2 * OWN, 2 * OWN)
                for i in range(FPZ):
                    v = jnp.concatenate([colbuf[yh_ * 2, c_, z_, i], colbuf[yh_ * 2 + 1, c_, z_, i]], axis=0)
                    hi, lo = split(v)
                    rhs[pl.ds(at, 2 * OWN), i * LANES : (i + 1) * LANES] = hi
                    rhs[pl.ds(n + at, 2 * OWN), i * LANES : (i + 1) * LANES] = lo
            return 0

        lax.fori_loop(0, 2, columns, 0)

    def products(c_, zs):
        n = len(zs) * WIDE
        both = mm(rhs[: 2 * n], lhs_hi[...])
        part = both[:n] + (both[n:] + mm(rhs[:n], lhs_lo[...]))
        for k, z_ in enumerate(zs):
            turned_gram[c_, z_] = part[k * WIDE : (k + 1) * WIDE].reshape(2, 2 * OWN, NZ * ROWS)

    own_cols.wait()
    prepare(c, range(NZ))
    all_arrived(rowbuf.at[pl.ds(0, 3)], x_r.at[0])
    for i in range(FPZ):
        rows = jnp.concatenate([rowbuf[:, (z + SLOT[j]) % NZ, i].reshape(ROWS, LANES) for j in range(NZ)], axis=0)
        hi, lo = split(rows.T)
        lhs_hi[pl.ds(i * LANES, LANES)] = hi
        lhs_lo[pl.ds(i * LANES, LANES)] = lo
    products(c, range(NZ))
    all_arrived(colbuf.at[pl.ds(0, 2), 0], c_r.at[0])
    part = [pairs[h] * 2 + u for h in range(2) for u in range(2)]
    prepare(1 - c, part)
    products(1 - c, part)
    all_arrived(colbuf.at[pl.ds(0, 2), 0], c_r.at[1])
    part = [pairs[h] * 2 + u for h in range(2, 4) for u in range(2)]
    prepare(1 - c, part)
    products(1 - c, part)
    get_window.wait()

    bit = iota((2 * OWN, LANES), 1) // 32

    def swap(a, b, n, shift):
        low = bit // n % 2 == 0
        return jnp.where(low, a, pltpu.roll(b, shift, 1)), jnp.where(low, pltpu.roll(a, LANES - shift, 1), b)

    def pack(g):
        for u in range(GP):
            es = [window[(g * GP + u) * PER + w] for w in range(PER)]
            for t in range(2):
                one = [
                    turned_gram[e_ % 2, e_ // 4, (e_ // 2) % 2, :, t * LANES : (t + 1) * LANES] for e_ in es
                ]
                even01, odd01 = swap(one[0], one[1], 1, 32)
                even23, odd23 = swap(one[2], one[3], 1, 32)
                by0, by2 = swap(even01, even23, 2, 64)
                by1, by3 = swap(odd01, odd23, 2, 64)
                for j, by in enumerate((by0, by1, by2, by3)):
                    pbuf[t * 4 + j, g * GP + u] = by

    def group(n):
        return (yl + 1 - n // 2) % 2 * 2 + (x // GP + 1 - n % 2) % 2

    def to_near(i, n):
        at = pl.ds(group(n) * GP, GP)
        if i < 2:
            return remote(
                pbuf.at[5 + i, at], near.at[i, at], n_s.at[0], n_r.at[n], dev(p, e_at((1, 7)[i]))
            )
        k = jnp.where(group(n) < NG // 2, 6, 2)
        return remote(pbuf.at[7, at], near.at[2, at], n_s.at[0], n_r.at[n], dev(p, e_at(k)))

    def block_to(j, n, u):
        back = SLOT.index(-SLOT[j] % NZ)
        p_ = group(n) * GP + u
        at = back * NP + (p_ + NP - p) % NP
        return remote(pbuf.at[j, p_], fin.at[at], f_s.at[0], f_r.at[0], dev(p_, e_at(SLOT[j])))

    def send_blocks(n, js):
        for u in range(GP):
            for j in js:
                if j:
                    block_to(j, n, u).start()
                else:

                    @pl.when(group(n) * GP + u != p)
                    def _():
                        block_to(j, n, u).start()

    def far_rows(n, _):
        pack(group(n))
        for i in (2, 0, 1):
            to_near(i, n).start()
        return 0

    def near_rows(n, _):
        send_blocks(n, (1, 2, 0))
        return 0

    def merge(n, _):
        at = pl.ds(group(n) * GP, GP)
        all_arrived(near.at[:, at], n_r.at[n])
        below = group(n) < NG // 2
        pbuf[3, at] = pbuf[3, at] + (near[0, at] + jnp.where(below, 0.0, near[2, at]))
        pbuf[4, at] = pbuf[4, at] + (near[1, at] + jnp.where(below, near[2, at], 0.0))
        send_blocks(n, (3, 4))
        return 0

    lax.fori_loop(0, NG, far_rows, 0)
    lax.fori_loop(0, NG, near_rows, 0)
    fin[0] = pbuf[0, p]
    lax.fori_loop(0, NG, merge, 0)
    all_arrived(fin.at[pl.ds(1, 5 * NP - 1)], f_r.at[0])

    def gram_from(p_):
        i = (p + NP - p_) % NP
        return (fin[i] + (fin[NP + i] + fin[2 * NP + i])) + (fin[3 * NP + i] + fin[4 * NP + i])

    gram = [gram_from(p_) for p_ in range(NP)]
    turned = jnp.concatenate(
        [
            gram[yl_ * NX + i][k * OWN : (k + 1) * OWN]
            for yl_ in range(2)
            for k in range(2)
            for i in range(NX)
        ],
        axis=0,
    ).T
    low = iota((ROWS, LANES), 1) < SEQ
    for t in range(2):
        a, b = turned[t * 64 : t * 64 + 32], turned[t * 64 + 32 : t * 64 + 64]
        out[:ROWS, t * LANES : (t + 1) * LANES] = jnp.where(low, a, pltpu.roll(b, SEQ, 1))
        out[ROWS:, t * LANES : (t + 1) * LANES] = jnp.where(low, pltpu.roll(a, SEQ, 1), b)
    all_sent(sbuf, a_s.at[0])
    all_sent(rowbuf.at[0, pl.ds(0, NZ - 1)], z_s.at[0])
    all_sent(rowbuf.at[pl.ds(0, 3)], x_s.at[0])
    all_sent(rowbuf.at[pl.ds(0, 3)], y_s.at[0])
    all_sent(rowbuf, c_s.at[0])
    all_sent(near, n_s.at[0])
    all_sent(fin.at[pl.ds(1, 5 * NP - 1)], f_s.at[0])


def per_device(acts, grads, positions, proj_in, proj_out, window):
    depth = acts.shape[2]
    vmem, dma = pltpu.VMEM, pltpu.SemaphoreType.DMA
    in_vmem, in_hbm = pl.BlockSpec(memory_space=pltpu.VMEM), pl.BlockSpec(memory_space=pltpu.HBM)
    tile = (NZ, FPZ, OWN, LANES)
    scratch = [
        vmem((LOSS, SEQ), jnp.int32),
        vmem((LANES, depth), BF16),
        vmem((NP, 2, OWN, LEN, depth), BF16),
        vmem((2, depth, LANES), BF16),
        vmem((NP, PICK, TOK), BF16),
        vmem((NP - 1, PICK, LANES), F32),
        vmem((NX, BY_Y, LANES), F32),
        vmem((2, NX, BY_X, LANES), F32),
        vmem((NX, BY_Y, LANES), F32),
        vmem((BY_X, LANES), F32),
        vmem((HALF, OWN, LANES), F32),
        vmem((NX, *tile), F32),
        vmem((NY, NC, *tile), F32),
        vmem((DEEP, NZ * ROWS), BF16),
        vmem((DEEP, NZ * ROWS), BF16),
        vmem((4 * NZ * 2 * OWN, DEEP), BF16),
        vmem((NC, NZ, 2, 2 * OWN, NZ * ROWS), F32),
        vmem((NZ, NP, 2 * OWN, LANES), F32),
        vmem((3, NP, 2 * OWN, LANES), F32),
        vmem((5 * NP, 2 * OWN, LANES), F32),
        pltpu.SMEM((WIN,), jnp.int32),
        pltpu.SemaphoreType.REGULAR, dma((3,)), dma((4,)),
        dma((1,)), dma((8,)), dma((1,)), dma((4,)), dma((1,)), dma((1,)),
        dma((1,)), dma((NY, PAIRS)), dma((1,)), dma((2,)), dma((1,)), dma((NG,)),
        dma((1,)), dma((1,)),
    ]
    operands = (acts, grads, positions.T, proj_in.T, proj_out.T, window)
    return pl.pallas_call(
        kernel,
        out_shape=jax.ShapeDtypeStruct((SEQ, 4 * SEQ), F32),
        in_specs=[in_hbm] * 6,
        out_specs=in_vmem,
        scratch_shapes=scratch,
        name="similarity",
        cost_estimate=pl.CostEstimate(flops=1_000_000_000, bytes_accessed=9_000_000, transcendentals=0),
        compiler_params=pltpu.CompilerParams(
            collective_id=0, has_side_effects=True, vmem_limit_bytes=40 << 20
        ),
    )(*(pltpu.with_memory_space_constraint(v, pltpu.HBM) for v in operands))


def solution(mesh):
    in_specs = (
        P("example", None, "param"),
        P("example", None, "param"),
        P("example", None),
        P("param", None),
        P("param", None),
        P(),
    )
    return jax.shard_map(
        per_device, mesh=mesh, in_specs=in_specs, out_specs=P("example", "param"), check_vma=False
    )
```
